32 devices in a mesh: dp: 8 (over z, core), space: 4 (over y, x).
Axes of the slice: x: 2, y: 2, z: 4, core: 2. Of those that a mesh axis runs over, the one named last changes fastest.
Arguments:
- features: bfloat16 [1024, 6272], P(('dp', 'space')), may hold values from -6 to 6
- grad_out: bfloat16 [1024, 6272], P(('dp', 'space')), may hold values from -6 to 6
- wigner: bfloat16 [455, 4096], P(None, ('dp', 'space')), may hold values from -1.5 to 1.5
- sources: int32 [4096], P(('dp', 'space')), may hold values from 0 to 47
- targets: int32 [4096], P(('dp', 'space')), may hold values from 0 to 31
- ghost_index: int32 [32, 2, 8], P(('dp', 'space')), may hold values from 0 to 31
- edge_count: int32 [8, 4], P('dp', 'space'), may hold values from 1 to 128, 384 in all within a row
- mixture: float32 [8, 32], replicated, may hold values from 0.25 to 2
- w_zero: bfloat16 [32, 896, 896], P('dp', 'space'), may hold values from -0.03125 to 0.03125
- w_one: bfloat16 [32, 2, 768, 768], P('dp', None, 'space'), may hold values from -0.02734375 to 0.02734375
- w_two: bfloat16 [32, 2, 640, 640], P('dp', None, 'space'), may hold values from -0.03125 to 0.03125
Outputs:
- updated: bfloat16 [1024, 6272], P(('dp', 'space'))
- grad_features: bfloat16 [1024, 6272], P(('dp', 'space'))
- grad_mix0: bfloat16 [8, 896, 896], P('dp', 'space')
- grad_mix1: bfloat16 [8, 2, 768, 768], P('dp', None, 'space')
- grad_mix2: bfloat16 [8, 2, 640, 640], P('dp', None, 'space')
The draws below stay inside these ranges and needn't reach their ends.
Inputs may be any that keep to these rules, and one draw needn't show every extreme that they name: `edge_count`: the counts of one system sum to 384, and some device of every system has all 128 slots live.
All inputs are finite; a program needn't handle non-finite values.
Results may differ from the reference program's by a relative error of at most 0.015.
Values may be sent and summed in bfloat16 or wider, within the bound.
No kernel may reach another device: no remote copies, remote signals or barrier semaphores. Data moves between devices by JAX's collectives and lax.ppermute only.
A program may use at most 128 MiB of HBM per device.

```python
import math
from functools import partial
import jax
import jax.numpy as jnp
import numpy as np
from jax import lax

CHANNELS = 128
LMAX = 6
MMAX = 2
EXPERTS = 32
ATOM_DEV = 32
EDGE_DEV = 128
GHOSTS = 8
NODE_W = 6272
WIG = 455
K0 = 896
K1 = 768
K2 = 640
PARAMS = 2801664
SYSTEMS = 8
ATOMS = 1024
EDGES = 4096
N_DP = 8
N_SPACE = 4
DEVICES = 32


def degree_tables():
    eyes = []
    spreads = []
    for degree in range(LMAX + 1):
        extent = 2 * degree + 1
        eyes.append(np.eye(extent, dtype=np.float32).reshape(-1))
        spreads.append(np.full(extent * extent, 0.6 / np.sqrt(extent), np.float32))
    return (np.concatenate(eyes)[:, None], np.concatenate(spreads)[:, None])


def draw_wigner(key, part):
    key = jax.random.fold_in(key, 11)
    diagonal, spread = degree_tables()
    first_key, second_key = jax.random.split(key)
    noise = jnp.clip(jax.random.normal(first_key, (WIG, EDGES), jnp.float32), -4.0, 4.0)
    center = jax.random.uniform(second_key, (WIG, EDGES), jnp.float32, 0.7, 1.3)
    value = jnp.asarray(diagonal) * center + (1.0 - jnp.asarray(diagonal)) * jnp.asarray(spread) * noise
    return value.astype(jnp.bfloat16)


def place_ends(array, own_key, low, largest):
    longest = array.shape.index(max(array.shape))
    spots = []
    for shift in (0, 1):
        where = [jax.random.randint(jax.random.fold_in(own_key, axis), (), 0, length) for axis, length in enumerate(array.shape)]
        where[longest] = (where[longest] + shift) % array.shape[longest]
        spots.append(tuple(where))
    return array.at[spots[0]].set(low).at[spots[1]].set(largest)


def steps_of(stream_key, shape, cuts, smallest, high):
    factor_of, own = 1.0, jax.random.fold_in(stream_key, 6)
    for axis_at, parts in cuts:
        draws = jnp.exp(jax.random.uniform(jax.random.fold_in(own, axis_at), (parts,), jnp.float32, smallest / len(cuts), high / len(cuts)))
        factor_of = factor_of * jnp.repeat(draws, shape[axis_at] // parts).reshape([-1 if axis == axis_at else 1 for axis in range(len(shape))])
    return factor_of


def length_profile(count, total, limit, lean):
    portions = [(1 << 20) // math.isqrt(rank ** lean) + 1 for rank in range(2, count + 1)]
    rest, given = total - limit - (count - 1), [1] * (count - 1)
    while rest > 0:
        candidates = [i for i in range(count - 1) if given[i] < limit]
        mass, remaining = sum([portions[i] for i in candidates]), rest
        for i in candidates:
            addition = min(limit - given[i], max(1, remaining * portions[i] // mass), rest)
            given[i] = given[i] + addition
            rest = rest - addition
    return np.array([limit] + given)


def uneven_parts(stream_key, count, total, limit, lean):
    if count == 2:
        one = jax.random.randint(stream_key, (), max(1, total - limit), min(limit, total - 1) + 1)
        return jnp.stack([one, total - one])
    lengths = jnp.asarray(length_profile(count, total, limit, lean), jnp.int32)
    pairs = (count - 1) // 2
    source_of, sink = lengths[1:1 + 2 * pairs:2], lengths[2:2 + 2 * pairs:2]
    slack = jnp.minimum(source_of - 1, limit - sink)
    moved = jax.random.randint(jax.random.fold_in(stream_key, 1), (pairs,), 0, 1 << 20) % (slack + 1)
    lengths = lengths.at[1:1 + 2 * pairs:2].set(source_of - moved).at[2:2 + 2 * pairs:2].set(sink + moved)
    return lengths[jax.random.permutation(jax.random.fold_in(stream_key, 2), count)]


def bell_draw(own_key, shape, scale, limit, cuts=(), kind=jnp.bfloat16):
    array = scale * jax.random.normal(own_key, shape, jnp.float32)
    if cuts:
        array = array * steps_of(own_key, shape, cuts, -0.22, 0.18)
    return jnp.clip(array, -limit, limit).astype(kind)


def setup_inputs(seed: int = 0) -> dict:
    key_of = jax.random.split(jax.random.key(seed), 12)
    return {
        "features": bell_draw(key_of[0], (ATOMS, NODE_W), 1.0, 6.0, ((0, 32),)),
        "grad_out": bell_draw(key_of[1], (ATOMS, NODE_W), 1.0, 6.0, ((0, 32),)),
        "wigner": draw_wigner(jax.random.fold_in(key_of[11], 71), 0),
        "sources": place_ends(jax.random.randint(key_of[3], (EDGES,), 0, ATOM_DEV + 2 * GHOSTS), jax.random.fold_in(key_of[3], 1), 0, (ATOM_DEV + 2 * GHOSTS) - 1).astype(jnp.int32),
        "targets": place_ends(jax.random.randint(key_of[4], (EDGES,), 0, ATOM_DEV), jax.random.fold_in(key_of[4], 1), 0, ATOM_DEV - 1).astype(jnp.int32),
        "ghost_index": place_ends(jax.random.randint(key_of[5], (DEVICES, 2, GHOSTS), 0, ATOM_DEV), jax.random.fold_in(key_of[5], 1), 0, ATOM_DEV - 1).astype(jnp.int32),
        "edge_count": jax.vmap(lambda own: uneven_parts(own, N_SPACE, 3 * N_SPACE * EDGE_DEV // 4, EDGE_DEV, 2))(jax.random.split(key_of[6], SYSTEMS)).reshape((SYSTEMS, N_SPACE)).astype(jnp.int32),
        "mixture": jnp.clip(jnp.exp(jax.random.uniform(key_of[7], (SYSTEMS, EXPERTS), jnp.float32, math.log(0.25), math.log(2.0))), 0.25, 2.0),
        "w_zero": bell_draw(key_of[8], (EXPERTS, K0, K0), (K0 * EXPERTS) ** -0.5, 0.03125, ((0, 8), (1, 4))),
        "w_one": bell_draw(key_of[9], (EXPERTS, 2, K1, K1), (2 * K1 * EXPERTS) ** -0.5, 0.02734375, ((0, 8), (2, 4))),
        "w_two": bell_draw(key_of[10], (EXPERTS, 2, K2, K2), (2 * K2 * EXPERTS) ** -0.5, 0.03125, ((0, 8), (2, 4))),
    }


message_scale = 0.25


def degree_start(degree):
    return degree * (2 * degree - 1) * (2 * degree + 1) // 3


def product_of(form, left_side, right_side):
    return jnp.einsum(form, left_side.astype(jnp.float32), right_side.astype(jnp.float32), precision=lax.Precision.HIGHEST)


def rotate_into(wigner, edge_rows):
    row_count = edge_rows.shape[0]
    blocks = []
    for degree in range(LMAX + 1):
        extent = 2 * degree + 1
        kept_order = min(degree, MMAX)
        offset = degree_start(degree)
        matrix = wigner[offset:offset + extent * extent].reshape(extent, extent, row_count)[degree - kept_order:degree + kept_order + 1]
        segment = edge_rows[:, degree * degree * CHANNELS:(degree + 1) * (degree + 1) * CHANNELS].reshape(row_count, extent, CHANNELS)
        blocks.append(product_of('jne,enc->ejc', matrix, segment).astype(jnp.bfloat16))
    return blocks


def rotate_back(wigner, blocks):
    row_count = blocks[0].shape[0]
    pieces = []
    for degree in range(LMAX + 1):
        extent = 2 * degree + 1
        kept_order = min(degree, MMAX)
        offset = degree_start(degree)
        matrix = wigner[offset:offset + extent * extent].reshape(extent, extent, row_count)[degree - kept_order:degree + kept_order + 1]
        pieces.append(product_of('jne,ejc->enc', matrix, blocks[degree]).reshape(row_count, extent * CHANNELS))
    return jnp.concatenate(pieces, 1)


def split_frame(blocks):
    row_count = blocks[0].shape[0]
    frame_zero = jnp.stack([blocks[d][:, min(d, MMAX)] for d in range(LMAX + 1)], 1).reshape(row_count, -1)
    frame_pairs = []
    for order_m in range(1, MMAX + 1):
        plus_part = jnp.stack([blocks[d][:, min(d, MMAX) + order_m] for d in range(order_m, LMAX + 1)], 1).reshape(row_count, -1)
        minus_part = jnp.stack([blocks[d][:, min(d, MMAX) - order_m] for d in range(order_m, LMAX + 1)], 1).reshape(row_count, -1)
        frame_pairs.append((plus_part, minus_part))
    return frame_zero, frame_pairs


def join_frame(frame_zero, frame_pairs):
    row_count = frame_zero.shape[0]
    zero_rows = frame_zero.reshape(row_count, LMAX + 1, CHANNELS)
    reshaped = [(p.reshape(row_count, -1, CHANNELS), q.reshape(row_count, -1, CHANNELS)) for p, q in frame_pairs]
    blocks = []
    for degree in range(LMAX + 1):
        kept_order = min(degree, MMAX)
        row_list = []
        for order_m in range(-kept_order, kept_order + 1):
            if order_m == 0:
                row_list.append(zero_rows[:, degree])
            elif order_m > 0:
                row_list.append(reshaped[order_m - 1][0][:, degree - order_m])
            else:
                row_list.append(reshaped[-order_m - 1][1][:, degree + order_m])
        blocks.append(jnp.stack(row_list, 1))
    return blocks


def convolve(frame_zero, frame_pairs, mix_set):
    out_zero = jnp.dot(frame_zero, mix_set[0], preferred_element_type=jnp.float32).astype(jnp.bfloat16)
    out_pairs = []
    for index_m, (plus_part, minus_part) in enumerate(frame_pairs):
        real_weight = mix_set[index_m + 1][0]
        imag_weight = mix_set[index_m + 1][1]
        out_plus = jnp.dot(plus_part, real_weight, preferred_element_type=jnp.float32) - jnp.dot(minus_part, imag_weight, preferred_element_type=jnp.float32)
        out_minus = jnp.dot(plus_part, imag_weight, preferred_element_type=jnp.float32) + jnp.dot(minus_part, real_weight, preferred_element_type=jnp.float32)
        out_pairs.append((out_plus.astype(jnp.bfloat16), out_minus.astype(jnp.bfloat16)))
    return out_zero, out_pairs


def transposed(left_side, right_side):
    return lax.dot_general(left_side, right_side, (((1,), (1,)), ((), ())), preferred_element_type=jnp.float32)


def outer_product(left_side, right_side):
    return lax.dot_general(left_side, right_side, (((0,), (0,)), ((), ())), preferred_element_type=jnp.float32)


def convolve_back(frame_zero, frame_pairs, mix_set):
    grad_zero = transposed(frame_zero, mix_set[0]).astype(jnp.bfloat16)
    grad_pairs = []
    for index_m, (plus_part, minus_part) in enumerate(frame_pairs):
        real_weight = mix_set[index_m + 1][0]
        imag_weight = mix_set[index_m + 1][1]
        grad_plus = transposed(plus_part, real_weight) + transposed(minus_part, imag_weight)
        grad_minus = transposed(minus_part, real_weight) - transposed(plus_part, imag_weight)
        grad_pairs.append((grad_plus.astype(jnp.bfloat16), grad_minus.astype(jnp.bfloat16)))
    return grad_zero, grad_pairs


def weight_terms(frame_zero, frame_pairs, back_zero, back_pairs, weight_scale):
    result = [(weight_scale * outer_product(frame_zero, back_zero))[None]]
    for (plus_part, minus_part), (back_plus, back_minus) in zip(frame_pairs, back_pairs):
        real_grad = outer_product(plus_part, back_plus) + outer_product(minus_part, back_minus)
        imag_grad = outer_product(plus_part, back_minus) - outer_product(minus_part, back_plus)
        result.append(weight_scale * jnp.stack([real_grad, imag_grad]))
    return tuple(result)


def take_rows(matrix, positions):
    return matrix[positions]


def add_rows(length, values, positions):
    return jnp.zeros((length, values.shape[1]), jnp.float32).at[positions].add(values)


def reference(features, grad_out, wigner, sources, targets, ghost_index, edge_count, mixture, w_zero, w_one, w_two):
    per_group = EXPERTS // N_DP
    experts_flat = jnp.concatenate([w_zero.reshape(EXPERTS, -1), w_one.reshape(EXPERTS, -1), w_two.reshape(EXPERTS, -1)], 1)
    grouped = experts_flat.astype(jnp.float32).reshape(N_DP, per_group, PARAMS)
    weight_scale = float(EDGE_DEV * N_SPACE) ** -0.5
    cut_one = K0 * K0
    cut_two = cut_one + 2 * K1 * K1
    table_rows = ATOM_DEV + 2 * GHOSTS
    slot_count = N_SPACE * EDGE_DEV

    def per_device(values):
        return values.reshape(N_SPACE, EDGE_DEV, -1)

    def one_system(inputs):
        feats_sys, gout_sys, wigner_sys, source_sys, target_sys, ghost_sys, count_sys, mix_row = inputs
        partial_mix = jnp.einsum('ge,gep->gp', mix_row.reshape(N_DP, per_group), grouped, precision=lax.Precision.HIGHEST)
        mixed = jnp.sum(lax.optimization_barrier(partial_mix.astype(jnp.bfloat16)).astype(jnp.float32), 0).astype(jnp.bfloat16)
        mix_set = (mixed[:cut_one].reshape(K0, K0), mixed[cut_one:cut_two].reshape(2, K1, K1), mixed[cut_two:].reshape(2, K2, K2))
        to_next = jax.vmap(take_rows)(feats_sys, ghost_sys[:, 0])
        to_prev = jax.vmap(take_rows)(feats_sys, ghost_sys[:, 1])
        node_table = jnp.concatenate([feats_sys, jnp.roll(to_next, 1, 0), jnp.roll(to_prev, -1, 0)], 1)
        edge_rows = jax.vmap(take_rows)(node_table, source_sys).reshape(slot_count, NODE_W)
        is_live = (jnp.arange(EDGE_DEV, dtype=jnp.int32)[None, :] < count_sys[:, None]).astype(jnp.float32)
        frame_zero, frame_pairs = split_frame(rotate_into(wigner_sys, edge_rows))
        out_zero, out_pairs = convolve(frame_zero, frame_pairs, mix_set)
        messages = rotate_back(wigner_sys, join_frame(out_zero, out_pairs)).astype(jnp.bfloat16)
        live_msgs = messages.reshape(N_SPACE, EDGE_DEV, NODE_W).astype(jnp.float32) * is_live[:, :, None]
        gathered = jax.vmap(partial(add_rows, ATOM_DEV))(live_msgs, target_sys)
        updated = (feats_sys.astype(jnp.float32) + message_scale * gathered).astype(jnp.bfloat16)
        picked = jax.vmap(take_rows)(gout_sys, target_sys).astype(jnp.float32)
        back_msg = (message_scale * picked * is_live[:, :, None]).astype(jnp.bfloat16).reshape(slot_count, NODE_W)
        back_zero, back_pairs = split_frame(rotate_into(wigner_sys, back_msg))
        grad_zero, grad_pairs = convolve_back(back_zero, back_pairs, mix_set)
        dev_pairs = [(per_device(p), per_device(q)) for p, q in frame_pairs]
        dev_back = [(per_device(p), per_device(q)) for p, q in back_pairs]
        dev_terms = jax.vmap(partial(weight_terms, weight_scale=weight_scale))(per_device(frame_zero), dev_pairs, per_device(back_zero), dev_back)
        sums = [jnp.sum(lax.optimization_barrier(term.astype(jnp.bfloat16)).astype(jnp.float32), 0).astype(jnp.bfloat16) for term in dev_terms]
        back_rows = rotate_back(wigner_sys, join_frame(grad_zero, grad_pairs)).astype(jnp.bfloat16)
        table_grad = jax.vmap(partial(add_rows, table_rows))(per_device(back_rows).astype(jnp.float32), source_sys)
        ghost_grad = lax.optimization_barrier(table_grad[:, ATOM_DEV:].astype(jnp.bfloat16)).astype(jnp.float32)
        from_next = jnp.roll(ghost_grad[:, :GHOSTS], -1, 0)
        from_prev = jnp.roll(ghost_grad[:, GHOSTS:], 1, 0)
        combined = gout_sys.astype(jnp.float32) + table_grad[:, :ATOM_DEV]
        combined = combined + jax.vmap(partial(add_rows, ATOM_DEV))(from_next, ghost_sys[:, 0])
        combined = combined + jax.vmap(partial(add_rows, ATOM_DEV))(from_prev, ghost_sys[:, 1])
        return updated, combined.astype(jnp.bfloat16), sums[0][0], sums[1], sums[2]

    inputs = (features.reshape(N_DP, N_SPACE, ATOM_DEV, NODE_W),
              grad_out.reshape(N_DP, N_SPACE, ATOM_DEV, NODE_W),
              jnp.moveaxis(wigner.reshape(WIG, N_DP, N_SPACE * EDGE_DEV), 1, 0),
              sources.reshape(N_DP, N_SPACE, EDGE_DEV),
              targets.reshape(N_DP, N_SPACE, EDGE_DEV),
              ghost_index.reshape(N_DP, N_SPACE, 2, GHOSTS),
              edge_count,
              mixture)
    updated, grad_features, grad_mix0, grad_mix1, grad_mix2 = lax.map(one_system, inputs)
    return (updated.reshape(ATOMS, NODE_W), grad_features.reshape(ATOMS, NODE_W), grad_mix0, grad_mix1, grad_mix2)
```

```python
import functools

import jax
import jax.numpy as jnp
from jax import lax
from jax.experimental import pallas as pl
from jax.experimental.pallas import tpu as pltpu
from jax.sharding import PartitionSpec as P

CHANNELS = 128
LMAX = 6
MMAX = 2
MESSAGE_SCALE = 0.25

BLOCK_COUNTS = (LMAX + 1, LMAX, LMAX, LMAX - 1, LMAX - 1)
FRAME_BLOCKS = sum(BLOCK_COUNTS)
FRAME_W = FRAME_BLOCKS * CHANNELS
COEFFS = (LMAX + 1) ** 2
NODE_W = COEFFS * CHANNELS

NN = (((1,), (0,)), ((), ()))
NT = (((1,), (1,)), ((), ()))
TN = (((0,), (0,)), ((), ()))

PARAMS = pltpu.CompilerParams(vmem_limit_bytes=48 * 1024 * 1024)
VMEM = pl.BlockSpec(memory_space=pltpu.VMEM)
SMEM = pl.BlockSpec(memory_space=pltpu.SMEM)
ANY = pl.BlockSpec(memory_space=pl.ANY)
HBM = pl.BlockSpec(memory_space=pltpu.HBM)


def dot(a, b, dims=NN):
    return lax.dot_general(a, b, dims, preferred_element_type=jnp.float32)


def degree_start(degree):
    return degree * (2 * degree - 1) * (2 * degree + 1) // 3


def frame_block(degree, order):
    if order == 0:
        return degree
    group = 2 * abs(order) - (1 if order > 0 else 0)
    return sum(BLOCK_COUNTS[:group]) + degree - abs(order)


def identity():
    rows = lax.broadcasted_iota(jnp.int32, (CHANNELS, CHANNELS), 0)
    cols = lax.broadcasted_iota(jnp.int32, (CHANNELS, CHANNELS), 1)
    return jnp.where(rows == cols, 1.0, 0.0).astype(jnp.bfloat16)


def mix_kernel(offset, other_offset, place_ref, mixture_ref, own_ref, other_ref, *refs):
    (both, across, here), (own, other, sems) = refs[:3], refs[3:]
    per_group, rows, width = own.shape
    outs = (both.at[:rows], both.at[rows:], across, here)
    blocks = sems.shape[1]
    block = rows // blocks
    copies = []
    for b in range(blocks):
        span = pl.ds(b * block, block)
        source = pl.ds(offset + b * block, block)
        copies.append(
            (
                pltpu.make_async_copy(own_ref.at[:, source, :], own.at[:, span, :], sems.at[0, b]),
                pltpu.make_async_copy(
                    other_ref.at[:, pl.ds(other_offset + b * block, block), :],
                    other.at[:, span, :],
                    sems.at[1, b],
                ),
            )
        )
    for pair in copies:
        for copy in pair:
            copy.start()
    dp = place_ref[0]
    z = dp // 2
    core = dp % 2
    beside = z + 1 - 2 * (z % 2)
    dests = (beside, 3 - beside, 3 - z, z)
    partner = dp + 1 - 2 * core
    coefs = []
    for dest in dests:
        system = 2 * dest + core
        coefs.append(
            [mixture_ref[system, dp * per_group + e] for e in range(per_group)]
            + [mixture_ref[system, partner * per_group + e] for e in range(per_group)]
        )

    def body(step, carry):
        row = pl.multiple_of(step * 16, 16)
        for column in range(0, width, CHANNELS):
            span = pl.ds(column, CHANNELS)
            parts = [own[e, pl.ds(row, 16), span].astype(jnp.float32) for e in range(per_group)]
            parts += [other[e, pl.ds(row, 16), span].astype(jnp.float32) for e in range(per_group)]
            for out, coef in zip(outs, coefs):
                total = coef[0] * parts[0]
                for c, part in zip(coef[1:], parts[1:]):
                    total = total + c * part
                out[pl.ds(row, 16), span] = total.astype(jnp.bfloat16)
        return carry

    for b, pair in enumerate(copies):
        for copy in pair:
            copy.wait()
        lax.fori_loop(b * block // 16, (b + 1) * block // 16, body, 0)


def mix(place, mixture, own, other, offset, other_offset, rows):
    per_group, _, width = other.shape
    blocks = 2 if rows % 32 == 0 else 1
    pair = jax.ShapeDtypeStruct((2 * rows, width), jnp.bfloat16)
    single = jax.ShapeDtypeStruct((rows, width), jnp.bfloat16)
    return pl.pallas_call(
        functools.partial(mix_kernel, offset, other_offset),
        in_specs=[SMEM, SMEM, HBM, ANY],
        out_specs=[VMEM] * 3,
        out_shape=[pair, single, single],
        scratch_shapes=[
            pltpu.VMEM((per_group, rows, width), jnp.bfloat16),
            pltpu.VMEM((per_group, rows, width), jnp.bfloat16),
            pltpu.SemaphoreType.DMA((2, blocks)),
        ],
        compiler_params=PARAMS,
        name="mix",
    )(place, mixture, pltpu.with_memory_space_constraint(own, pltpu.HBM), other)


def pick_kernel(index_ref, features_ref, next_ref, prev_ref):
    own = features_ref.shape[0]
    ghosts = index_ref.shape[2]
    columns = lax.broadcasted_iota(jnp.int32, (ghosts, own), 1)
    for place, out in ((0, next_ref), (1, prev_ref)):
        rows = lax.broadcasted_iota(jnp.int32, (ghosts, own), 0)
        wanted = jnp.zeros((ghosts, own), jnp.int32)
        for g in range(ghosts):
            wanted = jnp.where(rows == g, index_ref[0, place, g], wanted)
        hot = jnp.where(columns == wanted, 1.0, 0.0).astype(jnp.bfloat16)
        out[...] = dot(hot, features_ref[...]).astype(jnp.bfloat16)


def pick_ghosts(index, features):
    out = jax.ShapeDtypeStruct((index.shape[2], features.shape[1]), jnp.bfloat16)
    return pl.pallas_call(
        pick_kernel,
        in_specs=[SMEM, VMEM],
        out_specs=[VMEM] * 2,
        out_shape=[out, out],
        compiler_params=PARAMS,
        name="pick_ghosts",
    )(index, features)


def hot_rows(index, count, values=1.0, start=0):
    rows = lax.broadcasted_iota(jnp.int32, (count, index.shape[1]), 0) + start
    return jnp.where(index == rows, values, 0.0).astype(jnp.bfloat16)


def turn_into(wide, sources, targets):
    step_rows = 32

    def body(step, carry):
        base = pl.multiple_of(step * step_rows, step_rows)
        for degree in range(LMAX + 1):
            extent = 2 * degree + 1
            kept = min(degree, MMAX)
            for order in range(-kept, kept + 1):
                start = degree_start(degree) + extent * (degree + order)
                totals = [0.0] * len(sources)
                for n in range(extent):
                    row = pl.ds((degree * degree + n) * CHANNELS + base, step_rows)
                    factor = wide[pl.ds(start + n, 1), :]
                    totals = [t + factor * s[row, :] for t, s in zip(totals, sources)]
                place = pl.ds(frame_block(degree, order) * CHANNELS + base, step_rows)
                for target, total in zip(targets, totals):
                    target[place, :] = total.astype(jnp.bfloat16)
        return carry

    lax.fori_loop(0, CHANNELS // step_rows, body, 0)


BAND = 16


def packed_rows(own, wigner_rows, slab_rows):
    rotations = COEFFS * own
    targets = rotations + BAND * -(-wigner_rows // BAND)
    slab = targets + BAND
    return rotations, targets, slab, slab + slab_rows


def enter_kernel(
    place_ref, count_ref, features_ref, ghosts_ref, grad_ref, sources_ref, targets_ref, wigner_ref,
    frame_ref, back_ref, slab_ref, *rest,
):
    packs, (wide, forward, backward, turned, turned_back) = rest[:-5], rest[-5:]
    own = features_ref.shape[0]
    edges = sources_ref.shape[1]
    extra = ghosts_ref.shape[0]
    wig_rows = wigner_ref.shape[0]
    wide[...] = wigner_ref[...].astype(jnp.float32)
    sources = sources_ref[...]
    live = lax.broadcasted_iota(jnp.int32, (1, edges), 1) < count_ref[0, 0]
    targets = jnp.where(live, targets_ref[...], -1)
    from_own = hot_rows(sources, own)
    from_ghost = hot_rows(sources, extra, start=own)
    to_own = hot_rows(targets, own, MESSAGE_SCALE)
    for n in range(COEFFS):
        span = pl.ds(n * CHANNELS, CHANNELS)
        forward[span, :] = dot(features_ref[:, span], from_own, TN) + dot(
            ghosts_ref[:, span], from_ghost, TN
        )
        backward[span, :] = dot(grad_ref[:, span], to_own, TN)
    turn_into(wide, (forward, backward), (turned, turned_back))
    eye = identity()
    for k in range(FRAME_BLOCKS):
        span = pl.ds(k * CHANNELS, CHANNELS)
        frame_ref[:, span] = dot(eye, turned[span, :], NT).astype(jnp.bfloat16)
        back_ref[:, span] = dot(eye, turned_back[span, :], NT).astype(jnp.bfloat16)
    spaces = len(packs) + 1
    rotations_at, targets_at, slab_at, _ = packed_rows(own, wig_rows, slab_ref.shape[0])
    for peer in range(spaces):
        position = lax.bitwise_xor(place_ref[1], jnp.int32(peer))
        out, at = (slab_ref, 0) if peer == 0 else (packs[peer - 1], slab_at)
        first = 0
        for blocks in BLOCK_COUNTS:
            rows = blocks * CHANNELS // spaces
            begin = pl.multiple_of(first + position * rows, BAND)
            out[at : at + rows, :] = turned[pl.ds(begin, rows), :]
            at += rows
            first += blocks * CHANNELS
    padding = jnp.zeros((targets_at - rotations_at - wig_rows, edges), jnp.float32)
    rotations = jnp.concatenate([wide[...], padding], 0).astype(jnp.bfloat16)
    marks = jnp.broadcast_to(targets.astype(jnp.float32), (BAND, edges)).astype(jnp.bfloat16)
    for pack in packs:
        for n in range(COEFFS):
            pack[n * own : (n + 1) * own, :] = grad_ref[:, n * CHANNELS : (n + 1) * CHANNELS]
        pack[rotations_at:targets_at, :] = rotations
        pack[targets_at:slab_at, :] = marks


def enter(place, count, features, ghosts, grad_out, sources, targets, wigner, spaces):
    edges = sources.shape[1]
    frame = jax.ShapeDtypeStruct((edges, FRAME_W), jnp.bfloat16)
    slab = jax.ShapeDtypeStruct((FRAME_W // spaces, edges), jnp.bfloat16)
    pack_rows = packed_rows(features.shape[0], wigner.shape[0], FRAME_W // spaces)[-1]
    pack = jax.ShapeDtypeStruct((pack_rows, edges), jnp.bfloat16)
    return pl.pallas_call(
        enter_kernel,
        in_specs=[SMEM, SMEM] + [VMEM] * 6,
        out_specs=[VMEM] * (2 + spaces),
        out_shape=[frame, frame, slab] + [pack] * (spaces - 1),
        scratch_shapes=[
            pltpu.VMEM((wigner.shape[0], edges), jnp.float32),
            pltpu.VMEM((NODE_W, edges), jnp.float32),
            pltpu.VMEM((NODE_W, edges), jnp.float32),
            pltpu.VMEM((FRAME_W, edges), jnp.bfloat16),
            pltpu.VMEM((FRAME_W, edges), jnp.bfloat16),
        ],
        compiler_params=PARAMS,
        name="enter_frame",
    )(place, count, features, ghosts, grad_out, sources, targets, wigner)


def peer_frames_kernel(own, wig_rows, slab_rows, *refs):
    packs, (out, wide, backward, turned_back) = refs[:-4], refs[-4:]
    rotations_at, targets_at, slab_at, _ = packed_rows(own, wig_rows, slab_rows)
    eye = identity()
    for peer, pack in enumerate(packs):
        wide[...] = pack[rotations_at:targets_at, :].astype(jnp.float32)
        targets = pack[targets_at:slab_at, :].astype(jnp.float32)[:1].astype(jnp.int32)
        to_own = hot_rows(targets, own, MESSAGE_SCALE)
        for n in range(COEFFS):
            backward[n * CHANNELS : (n + 1) * CHANNELS, :] = dot(
                pack[n * own : (n + 1) * own, :], to_own, TN
            )
        turn_into(wide, (backward,), (turned_back,))
        for k in range(FRAME_BLOCKS):
            span = pl.ds(k * CHANNELS, CHANNELS)
            out[peer, :, span] = dot(eye, turned_back[span, :], NT).astype(jnp.bfloat16)


def peer_frames(packs, own, wig_rows, slab_rows):
    edges = packs[0].shape[1]
    return pl.pallas_call(
        functools.partial(peer_frames_kernel, own, wig_rows, slab_rows),
        in_specs=[VMEM] * len(packs),
        out_specs=VMEM,
        out_shape=jax.ShapeDtypeStruct((len(packs), edges, FRAME_W), jnp.bfloat16),
        scratch_shapes=[
            pltpu.VMEM((BAND * -(-wig_rows // BAND), edges), jnp.float32),
            pltpu.VMEM((NODE_W, edges), jnp.float32),
            pltpu.VMEM((FRAME_W, edges), jnp.bfloat16),
        ],
        compiler_params=PARAMS,
        name="peer_frames",
    )(*packs)


def weight_grad_kernel(scale, slab_ref, back_ref, backs, *refs):
    packs, (out_zero, out_one, out_two) = refs[:-3], refs[-3:]
    spaces = len(packs) + 1
    end = packs[0].shape[0]
    all_slabs = [slab_ref] + [pack.at[end - slab_ref.shape[0] : end] for pack in packs]
    all_backs = [back_ref] + [backs.at[k] for k in range(spaces - 1)]
    rows = [blocks * CHANNELS // spaces for blocks in BLOCK_COUNTS]
    widths = [blocks * CHANNELS for blocks in BLOCK_COUNTS]

    def product(a, b):
        left = slice(sum(rows[:a]), sum(rows[: a + 1]))
        right = slice(sum(widths[:b]), sum(widths[: b + 1]))
        return sum(dot(s[left, :], d[:, right]) for s, d in zip(all_slabs, all_backs))

    out_zero[...] = (scale * product(0, 0)).astype(jnp.bfloat16)
    for out, group in ((out_one, 1), (out_two, 3)):
        out[0] = (scale * (product(group, group) + product(group + 1, group + 1))).astype(jnp.bfloat16)
        out[1] = (scale * (product(group, group + 1) - product(group + 1, group))).astype(jnp.bfloat16)


def weight_grads(slab, back, backs, packs, scale):
    spaces = len(packs) + 1
    k0, k1, _, k2, _ = [blocks * CHANNELS for blocks in BLOCK_COUNTS]
    return pl.pallas_call(
        functools.partial(weight_grad_kernel, scale),
        in_specs=[VMEM] * (2 + spaces),
        out_specs=[VMEM] * 3,
        out_shape=[
            jax.ShapeDtypeStruct((k0 // spaces, k0), jnp.bfloat16),
            jax.ShapeDtypeStruct((2, k1 // spaces, k1), jnp.bfloat16),
            jax.ShapeDtypeStruct((2, k2 // spaces, k2), jnp.bfloat16),
        ],
        compiler_params=PARAMS,
        name="weight_grads",
    )(slab, back, backs, *packs)


def apply_kernel(group, places, local_rows, place_ref, frame_ref, back_ref, *refs):
    shards, (out_ref, grad_ref, full) = refs[:-3], refs[-3:]
    parts = 1 if group == 0 else 2
    for (peer, first_part, count, offset), shard in zip(places, shards):
        position = lax.bitwise_xor(place_ref[1], jnp.int32(peer))
        rows = shard.shape[0] // count
        begin = pl.multiple_of(position * local_rows + offset, 16)
        for k in range(count):
            full[first_part + k, pl.ds(begin, rows), :] = shard[k * rows : (k + 1) * rows, :]
    first = sum(BLOCK_COUNTS[:group]) * CHANNELS
    width = BLOCK_COUNTS[group] * CHANNELS
    eye = identity()
    edges = frame_ref.shape[0]

    def put_turned(value, offset):
        value = value.astype(jnp.bfloat16)
        for k in range(0, width, CHANNELS):
            out_ref[offset + k : offset + k + CHANNELS, :] = dot(
                eye, value[:, k : k + CHANNELS], NT
            ).astype(jnp.bfloat16)

    if parts == 1:
        grad_ref[...] = dot(full[0], back_ref[:, first : first + width], NT).astype(jnp.bfloat16)
        put_turned(dot(frame_ref[:, first : first + width], full[0]), 0)
        return
    second = first + width
    back = jnp.concatenate([back_ref[:, first:second], back_ref[:, second : second + width]], 0)
    real = dot(full[0], back, NT)
    imag = dot(full[1], back, NT)
    grad_ref[:width, :] = (real[:, :edges] + imag[:, edges:]).astype(jnp.bfloat16)
    grad_ref[width:, :] = (real[:, edges:] - imag[:, :edges]).astype(jnp.bfloat16)
    frame = jnp.concatenate([frame_ref[:, first:second], frame_ref[:, second : second + width]], 0)
    real = dot(frame, full[0])
    imag = dot(frame, full[1])
    put_turned(real[:edges] - imag[edges:], 0)
    put_turned(imag[:edges] + real[edges:], width)


def apply_weights(group, place, frame, back, pieces, spaces):
    places, shards = zip(*pieces)
    edges = frame.shape[0]
    width = BLOCK_COUNTS[group] * CHANNELS
    parts = 1 if group == 0 else 2
    out = jax.ShapeDtypeStruct((parts * width, edges), jnp.bfloat16)
    return pl.pallas_call(
        functools.partial(apply_kernel, group, places, width // spaces),
        in_specs=[SMEM] + [VMEM] * (2 + len(shards)),
        out_specs=[VMEM] * 2,
        out_shape=[out, out],
        scratch_shapes=[pltpu.VMEM((parts, width, width), jnp.bfloat16)],
        compiler_params=PARAMS,
        name=f"apply_weights_{group}",
    )(place, frame, back, *shards)


def leave(frames, wigner_ref, wide, turned):
    wide[...] = wigner_ref[...].astype(jnp.float32)
    step_rows = 32

    def body(step, carry):
        base = pl.multiple_of(step * step_rows, step_rows)
        for degree in range(LMAX + 1):
            extent = 2 * degree + 1
            kept = min(degree, MMAX)
            values = []
            for order in range(-kept, kept + 1):
                source = frames[abs(order)]
                block = degree - abs(order)
                if order < 0:
                    block += BLOCK_COUNTS[2 * -order]
                values.append(
                    source[pl.ds(block * CHANNELS + base, step_rows), :].astype(jnp.float32)
                )
            for n in range(extent):
                total = 0.0
                for order, value in zip(range(-kept, kept + 1), values):
                    start = degree_start(degree) + extent * (degree + order) + n
                    total = total + wide[pl.ds(start, 1), :] * value
                row = pl.ds((degree * degree + n) * CHANNELS + base, step_rows)
                turned[row, :] = total.astype(jnp.bfloat16)
        return carry

    lax.fori_loop(0, CHANNELS // step_rows, body, 0)


def leave_back_kernel(
    zero_ref, one_ref, two_ref, wigner_ref, sources_ref, grad_ref, base_ref, ghost_ref, wide, turned
):
    leave((zero_ref, one_ref, two_ref), wigner_ref, wide, turned)
    own = grad_ref.shape[0]
    extra = ghost_ref.shape[0]
    edges = sources_ref.shape[1]
    rows = lax.broadcasted_iota(jnp.int32, (own + extra, edges), 0)
    hot = jnp.where(sources_ref[...] == rows, 1.0, 0.0).astype(jnp.bfloat16)
    for n in range(COEFFS):
        span = pl.ds(n * CHANNELS, CHANNELS)
        table = dot(hot, turned[span, :], NT)
        base_ref[:, span] = grad_ref[:, span].astype(jnp.float32) + table[:own]
        ghost_ref[:, span] = table[own:].astype(jnp.bfloat16)


def leave_kernel(
    zero_ref, one_ref, two_ref, wigner_ref, count_ref, targets_ref, features_ref, out_ref, wide, turned
):
    leave((zero_ref, one_ref, two_ref), wigner_ref, wide, turned)
    own = features_ref.shape[0]
    edges = targets_ref.shape[1]
    rows = lax.broadcasted_iota(jnp.int32, (own, edges), 0)
    live = lax.broadcasted_iota(jnp.int32, (own, edges), 1) < count_ref[0, 0]
    hot = jnp.where((targets_ref[...] == rows) & live, MESSAGE_SCALE, 0.0).astype(jnp.bfloat16)
    for n in range(COEFFS):
        span = pl.ds(n * CHANNELS, CHANNELS)
        out_ref[:, span] = (
            features_ref[:, span].astype(jnp.float32) + dot(hot, turned[span, :], NT)
        ).astype(jnp.bfloat16)


def leave_scratch(wigner):
    rows, edges = wigner.shape
    return [pltpu.VMEM((rows, edges), jnp.float32), pltpu.VMEM((NODE_W, edges), jnp.bfloat16)]


def leave_back(frames, wigner, sources, grad_out, extra):
    own = grad_out.shape[0]
    return pl.pallas_call(
        leave_back_kernel,
        in_specs=[VMEM] * 6,
        out_specs=[VMEM] * 2,
        out_shape=[
            jax.ShapeDtypeStruct((own, NODE_W), jnp.float32),
            jax.ShapeDtypeStruct((extra, NODE_W), jnp.bfloat16),
        ],
        scratch_shapes=leave_scratch(wigner),
        compiler_params=PARAMS,
        name="leave_frame_back",
    )(*frames, wigner, sources, grad_out)


def leave_forward(frames, wigner, count, targets, features):
    return pl.pallas_call(
        leave_kernel,
        in_specs=[VMEM] * 4 + [SMEM] + [VMEM] * 2,
        out_specs=VMEM,
        out_shape=jax.ShapeDtypeStruct(features.shape, jnp.bfloat16),
        scratch_shapes=leave_scratch(wigner),
        compiler_params=PARAMS,
        name="leave_frame",
    )(*frames, wigner, count, targets, features)


def settle_kernel(base_ref, next_ref, prev_ref, index_ref, out_ref):
    own = base_ref.shape[0]
    ghosts = next_ref.shape[0]
    rows = lax.broadcasted_iota(jnp.int32, (own, ghosts), 0)
    total = base_ref[...]
    for place, ref in ((0, next_ref), (1, prev_ref)):
        hot = jnp.where(index_ref[place : place + 1, :] == rows, 1.0, 0.0)
        total = total + dot(hot, ref[...].astype(jnp.float32))
    out_ref[...] = total.astype(jnp.bfloat16)


def settle(base, from_next, from_prev, index):
    return pl.pallas_call(
        settle_kernel,
        in_specs=[VMEM] * 4,
        out_specs=VMEM,
        out_shape=jax.ShapeDtypeStruct(base.shape, jnp.bfloat16),
        compiler_params=PARAMS,
        name="settle_ghosts",
    )(base, from_next, from_prev, index)


def together(*values):
    return lax.optimization_barrier(values)


CORES = [(i, i ^ 1) for i in range(8)]
BESIDE = [(2 * z + c, 2 * (z ^ 1) + c) for z in range(4) for c in range(2)]
OPPOSITE = [(2 * z + c, 2 * (3 - z) + c) for z in range(4) for c in range(2)]


def add(*parts):
    return sum(part.astype(jnp.float32) for part in parts).astype(jnp.bfloat16)


def mixed_general(mixture, own):
    per_group = own.shape[0]
    columns = lax.dynamic_slice_in_dim(mixture, lax.axis_index("dp") * per_group, per_group, 1)
    sums = jnp.einsum(
        "se,erk->srk", columns, own.astype(jnp.float32), precision=lax.Precision.HIGHEST
    ).astype(jnp.bfloat16)
    return lax.psum_scatter(sums, "dp", scatter_dimension=0, tiled=False)


def to_peer(array, spaces, k):
    return lax.ppermute(array, "space", [(i, i ^ k) for i in range(spaces)])


def on_device(
    features,
    grad_out,
    wigner,
    sources,
    targets,
    ghost_index,
    edge_count,
    mixture,
    w_zero,
    w_one,
    w_two,
):
    edges = sources.shape[0]
    own_rows = features.shape[0]
    ghosts = ghost_index.shape[2]
    spaces = lax.axis_size("space")
    place = jnp.stack([lax.axis_index("dp"), lax.axis_index("space")]).astype(jnp.int32)
    up = [(i, (i + 1) % spaces) for i in range(spaces)]
    down = [(j, i) for i, j in up]
    per_group, rows_zero = w_zero.shape[:2]
    rows_one, rows_two = w_one.shape[2], w_two.shape[2]
    sources = sources.reshape(1, edges)
    targets = targets.reshape(1, edges)
    w_one = w_one.reshape(per_group, -1, w_one.shape[-1])
    w_two = w_two.reshape(per_group, -1, w_two.shape[-1])
    scale = float(edges * spaces) ** (-0.5)

    def frames(from_prev, from_next):
        return enter(
            place,
            edge_count,
            features,
            jnp.concatenate([from_prev, from_next], 0),
            grad_out,
            sources,
            targets,
            wigner,
            spaces,
        )

    to_next, to_prev = pick_ghosts(ghost_index, features)

    if lax.axis_size("dp") == 8 and spaces == 4:
        half = rows_zero // 2
        chunks = [
            (0, w_zero, 0, half, (0, 1, 0)),
            (3, w_two, 0, 2 * rows_two, (0, 2, 0)),
            (1, w_one, 0, rows_one, (0, 1, 0)),
            (1, w_one, rows_one, rows_one, (1, 1, 0)),
            (0, w_zero, half, rows_zero - half, (0, 1, half)),
        ]

        def swap_cores(array):
            return lax.ppermute(array, "dp", CORES)

        def mix_chunk(j, other, other_first=0):
            _, own, first, rows, _ = chunks[j]
            return mix(place, mixture, own, other, first, other_first, rows)

        def swap_beside(both):
            return lax.ppermute(both, "dp", BESIDE)

        def total_opposite(j, across, beside):
            return add(across, beside[chunks[j][3] :])

        def swap_opposite(total):
            return lax.ppermute(total, "dp", OPPOSITE)

        def total_here(j, here, beside, opposite):
            return add(here, beside[: chunks[j][3]], opposite)

        def to_sides(shard):
            return to_peer(shard, spaces, 1), to_peer(shard, spaces, 2)

        def forward(j, sides):
            along = 2 - j % 2
            return to_peer(sides[(3 ^ along) - 1], spaces, along)

        def pieces(j, shard, sides, last):
            return [((k,) + chunks[j][4], a) for k, a in enumerate((shard, *sides, last))]

        other0 = swap_cores(w_zero)
        other0, to_next, to_prev = together(other0, to_next, to_prev)
        both0, across0, here0 = mix_chunk(0, other0)
        beside0 = swap_beside(both0)
        from_prev = lax.ppermute(to_next, "space", up)
        from_next = lax.ppermute(to_prev, "space", down)
        sent, other0 = together(w_two, other0)
        other1 = swap_cores(sent)
        both1, across1, here1 = mix_chunk(1, other1)
        beside1 = swap_beside(both1)
        beside0, here1, from_prev, from_next = together(beside0, here1, from_prev, from_next)
        total0 = total_opposite(0, across0, beside0)
        opposite0 = swap_opposite(total0)
        sent, other1, here1 = together(w_one, other1, here1)
        other2 = swap_cores(sent)
        total0, from_prev, from_next = together(total0, from_prev, from_next)
        frame, back, slab, *packs = frames(from_prev, from_next)
        opposite0, frame = together(opposite0, frame)
        shard0 = total_here(0, here0, beside0, opposite0)
        shard0, packs[0], packs[1], other2 = together(shard0, packs[0], packs[1], other2)
        sides0 = to_sides(shard0)
        side_packs = [to_peer(packs[0], spaces, 1), to_peer(packs[1], spaces, 2)]
        other2, frame = together(other2, frame)
        both2, across2, here2 = mix_chunk(2, other2)
        beside2 = swap_beside(both2)
        both3, across3, here3 = mix_chunk(3, other2, rows_one)
        beside1, here2, here3, *sides0 = together(beside1, here2, here3, *sides0)
        total1 = total_opposite(1, across1, beside1)
        opposite1 = swap_opposite(total1)
        both3, beside2, here3 = together(both3, beside2, here3)
        beside3 = swap_beside(both3)
        total2 = total_opposite(2, across2, beside2)
        opposite2 = swap_opposite(total2)
        last_pack, total2, *side_packs = together(packs[2], total2, *side_packs)
        last_pack = to_peer(last_pack, spaces, 3)
        other0, total2 = together(other0, total2)
        both4, across4, here4 = mix_chunk(4, other0, half)
        opposite1, here4 = together(opposite1, here4)
        shard1 = total_here(1, here1, beside1, opposite1)
        shard1, *sides0 = together(shard1, *sides0)
        sides1 = to_sides(shard1)
        forward0 = forward(0, sides0)
        both4, beside3, here4, shard1 = together(both4, beside3, here4, shard1)
        beside4 = swap_beside(both4)
        total3 = total_opposite(3, across3, beside3)
        opposite3 = swap_opposite(total3)
        opposite2, total3 = together(opposite2, total3)
        shard2 = total_here(2, here2, beside2, opposite2)
        last_pack, shard2 = together(last_pack, shard2)
        packs_in = [*side_packs, last_pack]
        backs = peer_frames(packs_in, own_rows, wigner.shape[0], slab.shape[0])
        sides2 = to_sides(shard2)
        beside4, backs, *sides1 = together(beside4, backs, *sides1)
        forward1 = forward(1, sides1)
        total4 = total_opposite(4, across4, beside4)
        opposite4 = swap_opposite(total4)
        opposite3, total4 = together(opposite3, total4)
        shard3 = total_here(3, here3, beside3, opposite3)
        sides3 = to_sides(shard3)
        back, shard3 = together(back, shard3)
        grad_mix = weight_grads(slab, back, backs, packs_in, scale)
        opposite4, *grad_mix = together(opposite4, *grad_mix)
        opposite4, forward1, *sides2 = together(opposite4, forward1, *sides2)
        forward2 = forward(2, sides2)
        shard4 = total_here(4, here4, beside4, opposite4)
        sides4 = to_sides(shard4)
        outs, grads = {}, {}
        whole = {
            3: pieces(1, shard1, sides1, forward1),
            1: pieces(2, shard2, sides2, forward2) + pieces(3, shard3, sides3, forward(3, sides3)),
            0: pieces(0, shard0, sides0, forward0) + pieces(4, shard4, sides4, to_peer(shard4, spaces, 3)),
        }
    else:
        from_prev = lax.ppermute(to_next, "space", up)
        from_next = lax.ppermute(to_prev, "space", down)
        frame, back, slab, *packs = frames(from_prev, from_next)
        packs_in = [to_peer(pack, spaces, k + 1) for k, pack in enumerate(packs)]
        backs = peer_frames(packs_in, own_rows, wigner.shape[0], slab.shape[0])
        grad_mix = weight_grads(slab, back, backs, packs_in, scale)
        outs, grads, whole = {}, {}, {}
        for group, own, parts in ((3, w_two, 2), (1, w_one, 2), (0, w_zero, 1)):
            shard = mixed_general(mixture, own)
            whole[group] = [((0, 0, parts, 0), shard)] + [
                ((k, 0, parts, 0), to_peer(shard, spaces, k)) for k in range(1, spaces)
            ]

    for group, pieces_of in whole.items():
        outs[group], grads[group] = apply_weights(group, place, frame, back, pieces_of, spaces)
    base, returning = leave_back(
        [grads[g] for g in (0, 1, 3)], wigner, sources, grad_out, 2 * ghosts
    )
    back_next = lax.ppermute(returning[:ghosts], "space", down)
    back_prev = lax.ppermute(returning[ghosts:], "space", up)
    updated = leave_forward([outs[g] for g in (0, 1, 3)], wigner, edge_count, targets, features)
    grad_features = settle(base, back_next, back_prev, ghost_index[0])
    grad_mix0, grad_mix1, grad_mix2 = grad_mix
    return (updated, grad_features, grad_mix0[None], grad_mix1[None], grad_mix2[None])


def solution(mesh):
    return jax.shard_map(
        on_device,
        mesh=mesh,
        in_specs=(
            P(("dp", "space"), None),
            P(("dp", "space"), None),
            P(None, ("dp", "space")),
            P(("dp", "space")),
            P(("dp", "space")),
            P(("dp", "space"), None, None),
            P("dp", "space"),
            P(),
            P("dp", "space", None),
            P("dp", None, "space", None),
            P("dp", None, "space", None),
        ),
        out_specs=(
            P(("dp", "space"), None),
            P(("dp", "space"), None),
            P("dp", "space", None),
            P("dp", None, "space", None),
            P("dp", None, "space", None),
        ),
        check_vma=False,
    )
```

```python
import functools

import jax
import jax.numpy as jnp
from jax import lax
from jax.experimental import pallas as pl
from jax.experimental.pallas import tpu as pltpu
from jax.sharding import PartitionSpec as P

CHANNELS = 128
LMAX = 6
MMAX = 2
MESSAGE_SCALE = 0.25

BLOCK_COUNTS = (LMAX + 1, LMAX, LMAX, LMAX - 1, LMAX - 1)
FRAME_BLOCKS = sum(BLOCK_COUNTS)
FRAME_W = FRAME_BLOCKS * CHANNELS
COEFFS = (LMAX + 1) ** 2
NODE_W = COEFFS * CHANNELS

NN = (((1,), (0,)), ((), ()))
NT = (((1,), (1,)), ((), ()))
TN = (((0,), (0,)), ((), ()))

PARAMS = pltpu.CompilerParams(vmem_limit_bytes=48 * 1024 * 1024)
VMEM = pl.BlockSpec(memory_space=pltpu.VMEM)
SMEM = pl.BlockSpec(memory_space=pltpu.SMEM)
ANY = pl.BlockSpec(memory_space=pl.ANY)
HBM = pl.BlockSpec(memory_space=pltpu.HBM)


def dot(a, b, dims=NN):
    return lax.dot_general(a, b, dims, preferred_element_type=jnp.float32)


def degree_start(degree):
    return degree * (2 * degree - 1) * (2 * degree + 1) // 3


def frame_block(degree, order):
    if order == 0:
        return degree
    group = 2 * abs(order) - (1 if order > 0 else 0)
    return sum(BLOCK_COUNTS[:group]) + degree - abs(order)


def identity():
    rows = lax.broadcasted_iota(jnp.int32, (CHANNELS, CHANNELS), 0)
    cols = lax.broadcasted_iota(jnp.int32, (CHANNELS, CHANNELS), 1)
    return jnp.where(rows == cols, 1.0, 0.0).astype(jnp.bfloat16)


def mix_kernel(offset, other_offset, place_ref, mixture_ref, own_ref, other_ref, *refs):
    (both, across, here), (own, other, sems) = refs[:3], refs[3:]
    per_group, rows, width = own.shape
    outs = (both.at[:rows], both.at[rows:], across, here)
    blocks = sems.shape[1]
    block = rows // blocks
    copies = []
    for b in range(blocks):
        span = pl.ds(b * block, block)
        source = pl.ds(offset + b * block, block)
        copies.append(
            (
                pltpu.make_async_copy(own_ref.at[:, source, :], own.at[:, span, :], sems.at[0, b]),
                pltpu.make_async_copy(
                    other_ref.at[:, pl.ds(other_offset + b * block, block), :],
                    other.at[:, span, :],
                    sems.at[1, b],
                ),
            )
        )
    for pair in copies:
        for copy in pair:
            copy.start()
    dp = place_ref[0]
    z = dp // 2
    core = dp % 2
    beside = z + 1 - 2 * (z % 2)
    dests = (beside, 3 - beside, 3 - z, z)
    partner = dp + 1 - 2 * core
    coefs = []
    for dest in dests:
        system = 2 * dest + core
        coefs.append(
            [mixture_ref[system, dp * per_group + e] for e in range(per_group)]
            + [mixture_ref[system, partner * per_group + e] for e in range(per_group)]
        )

    def body(step, carry):
        row = pl.multiple_of(step * 16, 16)
        for column in range(0, width, CHANNELS):
            span = pl.ds(column, CHANNELS)
            parts = [own[e, pl.ds(row, 16), span].astype(jnp.float32) for e in range(per_group)]
            parts += [other[e, pl.ds(row, 16), span].astype(jnp.float32) for e in range(per_group)]
            for out, coef in zip(outs, coefs):
                total = coef[0] * parts[0]
                for c, part in zip(coef[1:], parts[1:]):
                    total = total + c * part
                out[pl.ds(row, 16), span] = total.astype(jnp.bfloat16)
        return carry

    for b, pair in enumerate(copies):
        for copy in pair:
            copy.wait()
        lax.fori_loop(b * block // 16, (b + 1) * block // 16, body, 0)


def mix(place, mixture, own, other, offset, other_offset, rows):
    per_group, _, width = other.shape
    blocks = 2 if rows % 32 == 0 else 1
    pair = jax.ShapeDtypeStruct((2 * rows, width), jnp.bfloat16)
    single = jax.ShapeDtypeStruct((rows, width), jnp.bfloat16)
    return pl.pallas_call(
        functools.partial(mix_kernel, offset, other_offset),
        in_specs=[SMEM, SMEM, HBM, ANY],
        out_specs=[VMEM] * 3,
        out_shape=[pair, single, single],
        scratch_shapes=[
            pltpu.VMEM((per_group, rows, width), jnp.bfloat16),
            pltpu.VMEM((per_group, rows, width), jnp.bfloat16),
            pltpu.SemaphoreType.DMA((2, blocks)),
        ],
        compiler_params=PARAMS,
        name="mix",
    )(place, mixture, pltpu.with_memory_space_constraint(own, pltpu.HBM), other)


def pick_kernel(index_ref, features_ref, next_ref, prev_ref):
    own = features_ref.shape[0]
    ghosts = index_ref.shape[2]
    columns = lax.broadcasted_iota(jnp.int32, (ghosts, own), 1)
    for place, out in ((0, next_ref), (1, prev_ref)):
        rows = lax.broadcasted_iota(jnp.int32, (ghosts, own), 0)
        wanted = jnp.zeros((ghosts, own), jnp.int32)
        for g in range(ghosts):
            wanted = jnp.where(rows == g, index_ref[0, place, g], wanted)
        hot = jnp.where(columns == wanted, 1.0, 0.0).astype(jnp.bfloat16)
        out[...] = dot(hot, features_ref[...]).astype(jnp.bfloat16)


def pick_ghosts(index, features):
    out = jax.ShapeDtypeStruct((index.shape[2], features.shape[1]), jnp.bfloat16)
    return pl.pallas_call(
        pick_kernel,
        in_specs=[SMEM, VMEM],
        out_specs=[VMEM] * 2,
        out_shape=[out, out],
        compiler_params=PARAMS,
        name="pick_ghosts",
    )(index, features)


def hot_rows(index, count, values=1.0, start=0):
    rows = lax.broadcasted_iota(jnp.int32, (count, index.shape[1]), 0) + start
    return jnp.where(index == rows, values, 0.0).astype(jnp.bfloat16)


def turn_into(wide, sources, targets):
    step_rows = 32

    def body(step, carry):
        base = pl.multiple_of(step * step_rows, step_rows)
        for degree in range(LMAX + 1):
            extent = 2 * degree + 1
            kept = min(degree, MMAX)
            for order in range(-kept, kept + 1):
                start = degree_start(degree) + extent * (degree + order)
                totals = [0.0] * len(sources)
                for n in range(extent):
                    row = pl.ds((degree * degree + n) * CHANNELS + base, step_rows)
                    factor = wide[pl.ds(start + n, 1), :]
                    totals = [t + factor * s[row, :] for t, s in zip(totals, sources)]
                place = pl.ds(frame_block(degree, order) * CHANNELS + base, step_rows)
                for target, total in zip(targets, totals):
                    target[place, :] = total.astype(jnp.bfloat16)
        return carry

    lax.fori_loop(0, CHANNELS // step_rows, body, 0)


BAND = 16


def packed_rows(own, wigner_rows):
    rotations = COEFFS * own
    targets = rotations + BAND * -(-wigner_rows // BAND)
    return rotations, targets, targets + BAND


def live_targets(count_ref, targets_ref):
    targets = targets_ref[...]
    live = lax.broadcasted_iota(jnp.int32, targets.shape, 1) < count_ref[0, 0]
    return jnp.where(live, targets, -1)


def pack_kernel(count_ref, grad_ref, targets_ref, wigner_ref, out_ref):
    own = grad_ref.shape[0]
    wig_rows, edges = wigner_ref.shape
    rotations_at, targets_at, end = packed_rows(own, wig_rows)
    for n in range(COEFFS):
        out_ref[n * own : (n + 1) * own, :] = grad_ref[:, n * CHANNELS : (n + 1) * CHANNELS]
    padding = jnp.zeros((targets_at - rotations_at - wig_rows, edges), jnp.float32)
    rotations = jnp.concatenate([wigner_ref[...].astype(jnp.float32), padding], 0)
    out_ref[rotations_at:targets_at, :] = rotations.astype(jnp.bfloat16)
    marks = live_targets(count_ref, targets_ref).astype(jnp.float32)
    out_ref[targets_at:end, :] = jnp.broadcast_to(marks, (BAND, edges)).astype(jnp.bfloat16)


def pack_inputs(count, grad_out, targets, wigner):
    rows = packed_rows(grad_out.shape[0], wigner.shape[0])[-1]
    return pl.pallas_call(
        pack_kernel,
        in_specs=[SMEM] + [VMEM] * 3,
        out_specs=VMEM,
        out_shape=jax.ShapeDtypeStruct((rows, wigner.shape[1]), jnp.bfloat16),
        compiler_params=PARAMS,
        name="pack_inputs",
    )(count, grad_out, targets, wigner)


def enter_kernel(
    place_ref, count_ref, features_ref, ghosts_ref, grad_ref, sources_ref, targets_ref, wigner_ref,
    frame_ref, back_ref, *rest,
):
    slabs, (wide, forward, backward, turned, turned_back) = rest[:-5], rest[-5:]
    own = features_ref.shape[0]
    extra = ghosts_ref.shape[0]
    wide[...] = wigner_ref[...].astype(jnp.float32)
    sources = sources_ref[...]
    targets = live_targets(count_ref, targets_ref)
    from_own = hot_rows(sources, own)
    from_ghost = hot_rows(sources, extra, start=own)
    to_own = hot_rows(targets, own, MESSAGE_SCALE)
    for n in range(COEFFS):
        span = pl.ds(n * CHANNELS, CHANNELS)
        forward[span, :] = dot(features_ref[:, span], from_own, TN) + dot(
            ghosts_ref[:, span], from_ghost, TN
        )
        backward[span, :] = dot(grad_ref[:, span], to_own, TN)
    turn_into(wide, (forward, backward), (turned, turned_back))
    eye = identity()
    for k in range(FRAME_BLOCKS):
        span = pl.ds(k * CHANNELS, CHANNELS)
        frame_ref[:, span] = dot(eye, turned[span, :], NT).astype(jnp.bfloat16)
        back_ref[:, span] = dot(eye, turned_back[span, :], NT).astype(jnp.bfloat16)
    spaces = len(slabs)
    for peer, slab in enumerate(slabs):
        position = lax.bitwise_xor(place_ref[1], jnp.int32(peer))
        at = first = 0
        for blocks in BLOCK_COUNTS:
            rows = blocks * CHANNELS // spaces
            begin = pl.multiple_of(first + position * rows, BAND)
            slab[at : at + rows, :] = turned[pl.ds(begin, rows), :]
            at += rows
            first += blocks * CHANNELS


def enter(place, count, features, ghosts, grad_out, sources, targets, wigner, spaces):
    edges = sources.shape[1]
    frame = jax.ShapeDtypeStruct((edges, FRAME_W), jnp.bfloat16)
    slab = jax.ShapeDtypeStruct((FRAME_W // spaces, edges), jnp.bfloat16)
    return pl.pallas_call(
        enter_kernel,
        in_specs=[SMEM, SMEM] + [VMEM] * 6,
        out_specs=[VMEM] * (2 + spaces),
        out_shape=[frame, frame] + [slab] * spaces,
        scratch_shapes=[
            pltpu.VMEM((wigner.shape[0], edges), jnp.float32),
            pltpu.VMEM((NODE_W, edges), jnp.float32),
            pltpu.VMEM((NODE_W, edges), jnp.float32),
            pltpu.VMEM((FRAME_W, edges), jnp.bfloat16),
            pltpu.VMEM((FRAME_W, edges), jnp.bfloat16),
        ],
        compiler_params=PARAMS,
        name="enter_frame",
    )(place, count, features, ghosts, grad_out, sources, targets, wigner)


def peer_frames_kernel(own, wig_rows, *refs):
    packs, (out, wide, backward, turned_back) = refs[:-4], refs[-4:]
    rotations_at, targets_at, end = packed_rows(own, wig_rows)
    eye = identity()
    for peer, pack in enumerate(packs):
        wide[...] = pack[rotations_at:targets_at, :].astype(jnp.float32)
        targets = pack[targets_at:end, :].astype(jnp.float32)[:1].astype(jnp.int32)
        to_own = hot_rows(targets, own, MESSAGE_SCALE)
        for n in range(COEFFS):
            backward[n * CHANNELS : (n + 1) * CHANNELS, :] = dot(
                pack[n * own : (n + 1) * own, :], to_own, TN
            )
        turn_into(wide, (backward,), (turned_back,))
        for k in range(FRAME_BLOCKS):
            span = pl.ds(k * CHANNELS, CHANNELS)
            out[peer, :, span] = dot(eye, turned_back[span, :], NT).astype(jnp.bfloat16)


def peer_frames(packs, own, wig_rows):
    edges = packs[0].shape[1]
    return pl.pallas_call(
        functools.partial(peer_frames_kernel, own, wig_rows),
        in_specs=[VMEM] * len(packs),
        out_specs=VMEM,
        out_shape=jax.ShapeDtypeStruct((len(packs), edges, FRAME_W), jnp.bfloat16),
        scratch_shapes=[
            pltpu.VMEM((BAND * -(-wig_rows // BAND), edges), jnp.float32),
            pltpu.VMEM((NODE_W, edges), jnp.float32),
            pltpu.VMEM((FRAME_W, edges), jnp.bfloat16),
        ],
        compiler_params=PARAMS,
        name="peer_frames",
    )(*packs)


def weight_grad_kernel(scale, back_ref, backs, *refs):
    all_slabs, (out_zero, out_one, out_two) = refs[:-3], refs[-3:]
    spaces = len(all_slabs)
    all_backs = [back_ref] + [backs.at[k] for k in range(spaces - 1)]
    rows = [blocks * CHANNELS // spaces for blocks in BLOCK_COUNTS]
    widths = [blocks * CHANNELS for blocks in BLOCK_COUNTS]

    def product(a, b):
        left = slice(sum(rows[:a]), sum(rows[: a + 1]))
        right = slice(sum(widths[:b]), sum(widths[: b + 1]))
        return sum(dot(s[left, :], d[:, right]) for s, d in zip(all_slabs, all_backs))

    out_zero[...] = (scale * product(0, 0)).astype(jnp.bfloat16)
    for out, group in ((out_one, 1), (out_two, 3)):
        out[0] = (scale * (product(group, group) + product(group + 1, group + 1))).astype(jnp.bfloat16)
        out[1] = (scale * (product(group, group + 1) - product(group + 1, group))).astype(jnp.bfloat16)


def weight_grads(back, backs, slabs, scale):
    spaces = len(slabs)
    k0, k1, _, k2, _ = [blocks * CHANNELS for blocks in BLOCK_COUNTS]
    return pl.pallas_call(
        functools.partial(weight_grad_kernel, scale),
        in_specs=[VMEM] * (2 + spaces),
        out_specs=[VMEM] * 3,
        out_shape=[
            jax.ShapeDtypeStruct((k0 // spaces, k0), jnp.bfloat16),
            jax.ShapeDtypeStruct((2, k1 // spaces, k1), jnp.bfloat16),
            jax.ShapeDtypeStruct((2, k2 // spaces, k2), jnp.bfloat16),
        ],
        compiler_params=PARAMS,
        name="weight_grads",
    )(back, backs, *slabs)


def apply_kernel(group, places, local_rows, place_ref, frame_ref, back_ref, *refs):
    shards, (out_ref, grad_ref, full) = refs[:-3], refs[-3:]
    parts = 1 if group == 0 else 2
    for (peer, first_part, count, offset, rows, at), shard in zip(places, shards):
        position = lax.bitwise_xor(place_ref[1], jnp.int32(peer))
        begin = pl.multiple_of(position * local_rows + offset, 16)
        for k in range(count):
            if at is None:
                full[first_part + k, pl.ds(begin, rows), :] = shard[k * rows : (k + 1) * rows, :]
                continue
            for column in range(BLOCK_COUNTS[group]):
                full[
                    first_part + k,
                    pl.ds(begin, rows),
                    column * CHANNELS : (column + 1) * CHANNELS,
                ] = shard[at : at + rows, :]
                at += rows
    first = sum(BLOCK_COUNTS[:group]) * CHANNELS
    width = BLOCK_COUNTS[group] * CHANNELS
    eye = identity()
    edges = frame_ref.shape[0]

    def put_turned(value, offset):
        value = value.astype(jnp.bfloat16)
        for k in range(0, width, CHANNELS):
            out_ref[offset + k : offset + k + CHANNELS, :] = dot(
                eye, value[:, k : k + CHANNELS], NT
            ).astype(jnp.bfloat16)

    if parts == 1:
        grad_ref[...] = dot(full[0], back_ref[:, first : first + width], NT).astype(jnp.bfloat16)
        put_turned(dot(frame_ref[:, first : first + width], full[0]), 0)
        return
    second = first + width
    back = jnp.concatenate([back_ref[:, first:second], back_ref[:, second : second + width]], 0)
    real = dot(full[0], back, NT)
    imag = dot(full[1], back, NT)
    grad_ref[:width, :] = (real[:, :edges] + imag[:, edges:]).astype(jnp.bfloat16)
    grad_ref[width:, :] = (real[:, edges:] - imag[:, :edges]).astype(jnp.bfloat16)
    frame = jnp.concatenate([frame_ref[:, first:second], frame_ref[:, second : second + width]], 0)
    real = dot(frame, full[0])
    imag = dot(frame, full[1])
    put_turned(real[:edges] - imag[edges:], 0)
    put_turned(imag[:edges] + real[edges:], width)


def apply_weights(group, place, frame, back, pieces, spaces):
    places, shards = zip(*pieces)
    edges = frame.shape[0]
    width = BLOCK_COUNTS[group] * CHANNELS
    parts = 1 if group == 0 else 2
    out = jax.ShapeDtypeStruct((parts * width, edges), jnp.bfloat16)
    return pl.pallas_call(
        functools.partial(apply_kernel, group, places, width // spaces),
        in_specs=[SMEM] + [VMEM] * (2 + len(shards)),
        out_specs=[VMEM] * 2,
        out_shape=[out, out],
        scratch_shapes=[pltpu.VMEM((parts, width, width), jnp.bfloat16)],
        compiler_params=PARAMS,
        name=f"apply_weights_{group}",
    )(place, frame, back, *shards)


def finish_kernel(*refs):
    out = refs[-1]
    at = 0
    for here, beside, opposite in zip(refs[:-1:3], refs[1:-1:3], refs[2:-1:3]):
        rows, width = here.shape
        step = rows if rows < 160 else rows // 2
        for first in range(0, rows, step):
            span = slice(first, first + step)
            for column in range(0, width, CHANNELS):
                lanes = slice(column, column + CHANNELS)
                total = sum(r[span, lanes].astype(jnp.float32) for r in (here, beside, opposite))
                out[at : at + step, :] = total.astype(jnp.bfloat16)
                at += step


def finish(*chunks):
    arrays = [array for chunk in chunks for array in chunk]
    rows = sum(here.size // CHANNELS for here, _, _ in chunks)
    return pl.pallas_call(
        finish_kernel,
        in_specs=[VMEM] * len(arrays),
        out_specs=VMEM,
        out_shape=jax.ShapeDtypeStruct((rows, CHANNELS), jnp.bfloat16),
        compiler_params=PARAMS,
        name="finish_first",
    )(*arrays)


def leave(frames, wigner_ref, wide, turned):
    wide[...] = wigner_ref[...].astype(jnp.float32)
    step_rows = 32

    def body(step, carry):
        base = pl.multiple_of(step * step_rows, step_rows)
        for degree in range(LMAX + 1):
            extent = 2 * degree + 1
            kept = min(degree, MMAX)
            values = []
            for order in range(-kept, kept + 1):
                source = frames[abs(order)]
                block = degree - abs(order)
                if order < 0:
                    block += BLOCK_COUNTS[2 * -order]
                values.append(
                    source[pl.ds(block * CHANNELS + base, step_rows), :].astype(jnp.float32)
                )
            for n in range(extent):
                total = 0.0
                for order, value in zip(range(-kept, kept + 1), values):
                    start = degree_start(degree) + extent * (degree + order) + n
                    total = total + wide[pl.ds(start, 1), :] * value
                row = pl.ds((degree * degree + n) * CHANNELS + base, step_rows)
                turned[row, :] = total.astype(jnp.bfloat16)
        return carry

    lax.fori_loop(0, CHANNELS // step_rows, body, 0)


def leave_back_kernel(
    zero_ref, one_ref, two_ref, wigner_ref, sources_ref, grad_ref, base_ref, ghost_ref, wide, turned
):
    leave((zero_ref, one_ref, two_ref), wigner_ref, wide, turned)
    own = grad_ref.shape[0]
    extra = ghost_ref.shape[0]
    edges = sources_ref.shape[1]
    rows = lax.broadcasted_iota(jnp.int32, (own + extra, edges), 0)
    hot = jnp.where(sources_ref[...] == rows, 1.0, 0.0).astype(jnp.bfloat16)
    for n in range(COEFFS):
        span = pl.ds(n * CHANNELS, CHANNELS)
        table = dot(hot, turned[span, :], NT)
        base_ref[:, span] = grad_ref[:, span].astype(jnp.float32) + table[:own]
        ghost_ref[:, span] = table[own:].astype(jnp.bfloat16)


def leave_kernel(
    zero_ref, one_ref, two_ref, wigner_ref, count_ref, targets_ref, features_ref, out_ref, wide, turned
):
    leave((zero_ref, one_ref, two_ref), wigner_ref, wide, turned)
    own = features_ref.shape[0]
    edges = targets_ref.shape[1]
    rows = lax.broadcasted_iota(jnp.int32, (own, edges), 0)
    live = lax.broadcasted_iota(jnp.int32, (own, edges), 1) < count_ref[0, 0]
    hot = jnp.where((targets_ref[...] == rows) & live, MESSAGE_SCALE, 0.0).astype(jnp.bfloat16)
    for n in range(COEFFS):
        span = pl.ds(n * CHANNELS, CHANNELS)
        out_ref[:, span] = (
            features_ref[:, span].astype(jnp.float32) + dot(hot, turned[span, :], NT)
        ).astype(jnp.bfloat16)


def leave_scratch(wigner):
    rows, edges = wigner.shape
    return [pltpu.VMEM((rows, edges), jnp.float32), pltpu.VMEM((NODE_W, edges), jnp.bfloat16)]


def leave_back(frames, wigner, sources, grad_out, extra):
    own = grad_out.shape[0]
    return pl.pallas_call(
        leave_back_kernel,
        in_specs=[VMEM] * 6,
        out_specs=[VMEM] * 2,
        out_shape=[
            jax.ShapeDtypeStruct((own, NODE_W), jnp.float32),
            jax.ShapeDtypeStruct((extra, NODE_W), jnp.bfloat16),
        ],
        scratch_shapes=leave_scratch(wigner),
        compiler_params=PARAMS,
        name="leave_frame_back",
    )(*frames, wigner, sources, grad_out)


def leave_forward(frames, wigner, count, targets, features):
    return pl.pallas_call(
        leave_kernel,
        in_specs=[VMEM] * 4 + [SMEM] + [VMEM] * 2,
        out_specs=VMEM,
        out_shape=jax.ShapeDtypeStruct(features.shape, jnp.bfloat16),
        scratch_shapes=leave_scratch(wigner),
        compiler_params=PARAMS,
        name="leave_frame",
    )(*frames, wigner, count, targets, features)


def settle_kernel(base_ref, next_ref, prev_ref, index_ref, out_ref):
    own = base_ref.shape[0]
    ghosts = next_ref.shape[0]
    rows = lax.broadcasted_iota(jnp.int32, (own, ghosts), 0)
    total = base_ref[...]
    for place, ref in ((0, next_ref), (1, prev_ref)):
        hot = jnp.where(index_ref[place : place + 1, :] == rows, 1.0, 0.0)
        total = total + dot(hot, ref[...].astype(jnp.float32))
    out_ref[...] = total.astype(jnp.bfloat16)


def settle(base, from_next, from_prev, index):
    return pl.pallas_call(
        settle_kernel,
        in_specs=[VMEM] * 4,
        out_specs=VMEM,
        out_shape=jax.ShapeDtypeStruct(base.shape, jnp.bfloat16),
        compiler_params=PARAMS,
        name="settle_ghosts",
    )(base, from_next, from_prev, index)


def together(*values):
    return lax.optimization_barrier(values)


CORES = [(i, i ^ 1) for i in range(8)]
BESIDE = [(2 * z + c, 2 * (z ^ 1) + c) for z in range(4) for c in range(2)]
OPPOSITE = [(2 * z + c, 2 * (3 - z) + c) for z in range(4) for c in range(2)]


def add(*parts):
    return sum(part.astype(jnp.float32) for part in parts).astype(jnp.bfloat16)


def mixed_general(mixture, own):
    per_group = own.shape[0]
    columns = lax.dynamic_slice_in_dim(mixture, lax.axis_index("dp") * per_group, per_group, 1)
    sums = jnp.einsum(
        "se,erk->srk", columns, own.astype(jnp.float32), precision=lax.Precision.HIGHEST
    ).astype(jnp.bfloat16)
    return lax.psum_scatter(sums, "dp", scatter_dimension=0, tiled=False)


def to_peer(array, spaces, k):
    return lax.ppermute(array, "space", [(i, i ^ k) for i in range(spaces)])


def on_device(
    features,
    grad_out,
    wigner,
    sources,
    targets,
    ghost_index,
    edge_count,
    mixture,
    w_zero,
    w_one,
    w_two,
):
    edges = sources.shape[0]
    own_rows = features.shape[0]
    ghosts = ghost_index.shape[2]
    spaces = lax.axis_size("space")
    place = jnp.stack([lax.axis_index("dp"), lax.axis_index("space")]).astype(jnp.int32)
    up = [(i, (i + 1) % spaces) for i in range(spaces)]
    down = [(j, i) for i, j in up]
    per_group, rows_zero = w_zero.shape[:2]
    rows_one, rows_two = w_one.shape[2], w_two.shape[2]
    sources = sources.reshape(1, edges)
    targets = targets.reshape(1, edges)
    w_one = w_one.reshape(per_group, -1, w_one.shape[-1])
    w_two = w_two.reshape(per_group, -1, w_two.shape[-1])
    scale = float(edges * spaces) ** (-0.5)

    def frames(from_prev, from_next):
        return enter(
            place,
            edge_count,
            features,
            jnp.concatenate([from_prev, from_next], 0),
            grad_out,
            sources,
            targets,
            wigner,
            spaces,
        )

    to_next, to_prev = pick_ghosts(ghost_index, features)

    if lax.axis_size("dp") == 8 and spaces == 4:
        half = rows_zero // 2
        chunks = [
            (0, w_zero, 0, half, (0, 1, 0)),
            (3, w_two, 0, 2 * rows_two, (0, 2, 0)),
            (1, w_one, 0, rows_one, (0, 1, 0)),
            (1, w_one, rows_one, rows_one, (1, 1, 0)),
            (0, w_zero, half, rows_zero - half, (0, 1, half)),
        ]

        def swap_cores(array):
            return lax.ppermute(array, "dp", CORES)

        def mix_chunk(j, other, other_first=0):
            _, own, first, rows, _ = chunks[j]
            return mix(place, mixture, own, other, first, other_first, rows)

        def swap_beside(both):
            return lax.ppermute(both, "dp", BESIDE)

        def total_opposite(j, across, beside):
            return add(across, beside[chunks[j][3] :])

        def swap_opposite(total):
            return lax.ppermute(total, "dp", OPPOSITE)

        def total_here(j, here, beside, opposite):
            return add(here, beside[: chunks[j][3]], opposite)

        def to_sides(shard):
            return to_peer(shard, spaces, 1), to_peer(shard, spaces, 2)

        def forward(j, sides):
            along = 1 if j == 1 else 2
            return to_peer(sides[(3 ^ along) - 1], spaces, along)

        def pieces(j, shard, sides, last, at=None):
            _, _, _, rows, (part, parts, offset) = chunks[j]
            return [
                ((k, part, parts, offset, rows // parts, at), a)
                for k, a in enumerate((shard, *sides, last))
            ]

        other0 = swap_cores(w_zero)
        other0, to_next, to_prev = together(other0, to_next, to_prev)
        both0, across0, here0 = mix_chunk(0, other0)
        beside0 = swap_beside(both0)
        from_prev = lax.ppermute(to_next, "space", up)
        from_next = lax.ppermute(to_prev, "space", down)
        sent, other0 = together(w_two, other0)
        other1 = swap_cores(sent)
        raw = pack_inputs(edge_count, grad_out, targets, wigner)
        raws = [to_peer(raw, spaces, 1), to_peer(raw, spaces, 2)]
        both1, across1, here1 = mix_chunk(1, other1)
        beside1 = swap_beside(both1)
        beside0, here1, from_prev, from_next = together(beside0, here1, from_prev, from_next)
        total0 = total_opposite(0, across0, beside0)
        opposite0 = swap_opposite(total0)
        sent, other1, here1 = together(w_one, other1, here1)
        other2 = swap_cores(sent)
        total0, from_prev, from_next = together(total0, from_prev, from_next)
        frame, back, *slabs = frames(from_prev, from_next)
        slabs[1], slabs[2], other2, opposite0 = together(slabs[1], slabs[2], other2, opposite0)
        slabs[1], slabs[2] = to_peer(slabs[1], spaces, 1), to_peer(slabs[2], spaces, 2)
        raw, frame, *raws = together(raw, frame, *raws)
        raws.append(to_peer(raw, spaces, 3))
        other2, frame = together(other2, frame)
        both2, across2, here2 = mix_chunk(2, other2)
        beside2 = swap_beside(both2)
        both3, across3, here3 = mix_chunk(3, other2, rows_one)
        here3, raws[2] = together(here3, raws[2])
        backs = peer_frames(raws, own_rows, wigner.shape[0])
        beside1, here2, here3, backs = together(beside1, here2, here3, backs)
        total1 = total_opposite(1, across1, beside1)
        opposite1 = swap_opposite(total1)
        other0, beside1 = together(other0, beside1)
        both4, across4, here4 = mix_chunk(4, other0, half)
        both3, beside2, here4 = together(both3, beside2, here4)
        beside3 = swap_beside(both3)
        total2 = total_opposite(2, across2, beside2)
        opposite2 = swap_opposite(total2)
        beside2, *slabs[1:] = together(beside2, *slabs[1:])
        slabs[3] = to_peer(slabs[3], spaces, 3)
        opposite1, beside2 = together(opposite1, beside2)
        shard1 = finish((here0, beside0, opposite0), (here1, beside1, opposite1))
        sides1 = to_sides(shard1)
        both4, beside3, shard1 = together(both4, beside3, shard1)
        beside4 = swap_beside(both4)
        total3 = total_opposite(3, across3, beside3)
        opposite3 = swap_opposite(total3)
        shard2 = total_here(2, here2, beside2, opposite2)
        shard2, *sides1 = together(shard2, *sides1)
        forward1 = forward(1, sides1)
        sides2 = to_sides(shard2)
        beside4, shard2, slabs[3] = together(beside4, shard2, slabs[3])
        total4 = total_opposite(4, across4, beside4)
        opposite4 = swap_opposite(total4)
        opposite3, total4 = together(opposite3, total4)
        shard3 = total_here(3, here3, beside3, opposite3)
        sides3 = to_sides(shard3)
        opposite4, *sides2 = together(opposite4, *sides2)
        shard4 = total_here(4, here4, beside4, opposite4)
        late_back, shard4, slabs[3] = together(back, shard4, slabs[3])
        grad_mix = weight_grads(late_back, backs, slabs, scale)
        sides4 = to_sides(shard4)
        forward2 = forward(2, sides2)
        shard4 = total_here(4, here4, beside4, opposite4)
        late_back, shard4, slabs[3] = together(back, shard4, slabs[3])
        grad_mix = weight_grads(late_back, backs, slabs, scale)
        sides4 = to_sides(shard4)
        outs, grads = {}, {}
        whole = {
            3: pieces(1, shard1, sides1, forward1, half * BLOCK_COUNTS[0]),
            1: pieces(2, shard2, sides2, forward2) + pieces(3, shard3, sides3, forward(3, sides3)),
            0: pieces(0, shard1, sides1, forward1, 0) + pieces(4, shard4, sides4, to_peer(shard4, spaces, 3)),
        }
    else:
        from_prev = lax.ppermute(to_next, "space", up)
        from_next = lax.ppermute(to_prev, "space", down)
        frame, back, *slabs = frames(from_prev, from_next)
        slabs = [slabs[0]] + [to_peer(slabs[k], spaces, k) for k in range(1, spaces)]
        raw = pack_inputs(edge_count, grad_out, targets, wigner)
        raws = [to_peer(raw, spaces, k) for k in range(1, spaces)]
        backs = peer_frames(raws, own_rows, wigner.shape[0])
        grad_mix = weight_grads(back, backs, slabs, scale)
        outs, grads, whole = {}, {}, {}
        for group, own, parts in ((3, w_two, 2), (1, w_one, 2), (0, w_zero, 1)):
            shard = mixed_general(mixture, own)
            rows = shard.shape[0] // parts

            def place_of(k):
                return (k, 0, parts, 0, rows, None)

            whole[group] = [(place_of(0), shard)] + [
                (place_of(k), to_peer(shard, spaces, k)) for k in range(1, spaces)
            ]

    for group, pieces_of in whole.items():
        if group == 0:
            frame, grads[1], *grad_mix = together(frame, grads[1], *grad_mix)
        outs[group], grads[group] = apply_weights(group, place, frame, back, pieces_of, spaces)
    base, returning = leave_back(
        [grads[g] for g in (0, 1, 3)], wigner, sources, grad_out, 2 * ghosts
    )
    back_next = lax.ppermute(returning[:ghosts], "space", down)
    back_prev = lax.ppermute(returning[ghosts:], "space", up)
    updated = leave_forward([outs[g] for g in (0, 1, 3)], wigner, edge_count, targets, features)
    grad_features = settle(base, back_next, back_prev, ghost_index[0])
    grad_mix0, grad_mix1, grad_mix2 = grad_mix
    return (updated, grad_features, grad_mix0[None], grad_mix1[None], grad_mix2[None])


def solution(mesh):
    return jax.shard_map(
        on_device,
        mesh=mesh,
        in_specs=(
            P(("dp", "space"), None),
            P(("dp", "space"), None),
            P(None, ("dp", "space")),
            P(("dp", "space")),
            P(("dp", "space")),
            P(("dp", "space"), None, None),
            P("dp", "space"),
            P(),
            P("dp", "space", None),
            P("dp", None, "space", None),
            P("dp", None, "space", None),
        ),
        out_specs=(
            P(("dp", "space"), None),
            P(("dp", "space"), None),
            P("dp", "space", None),
            P("dp", None, "space", None),
            P("dp", None, "space", None),
        ),
        check_vma=False,
    )
```

```python
import functools

import jax
import jax.numpy as jnp
from jax import lax
from jax.experimental import pallas as pl
from jax.experimental.pallas import tpu as pltpu
from jax.sharding import PartitionSpec as P

CHANNELS = 128
LMAX = 6
MMAX = 2
MESSAGE_SCALE = 0.25

BLOCK_COUNTS = (LMAX + 1, LMAX, LMAX, LMAX - 1, LMAX - 1)
FRAME_BLOCKS = sum(BLOCK_COUNTS)
FRAME_W = FRAME_BLOCKS * CHANNELS
COEFFS = (LMAX + 1) ** 2
NODE_W = COEFFS * CHANNELS

NN = (((1,), (0,)), ((), ()))
NT = (((1,), (1,)), ((), ()))
TN = (((0,), (0,)), ((), ()))

PARAMS = pltpu.CompilerParams(vmem_limit_bytes=48 * 1024 * 1024)
VMEM = pl.BlockSpec(memory_space=pltpu.VMEM)
SMEM = pl.BlockSpec(memory_space=pltpu.SMEM)
ANY = pl.BlockSpec(memory_space=pl.ANY)
HBM = pl.BlockSpec(memory_space=pltpu.HBM)


def dot(a, b, dims=NN):
    return lax.dot_general(a, b, dims, preferred_element_type=jnp.float32)


def degree_start(degree):
    return degree * (2 * degree - 1) * (2 * degree + 1) // 3


def frame_block(degree, order):
    if order == 0:
        return degree
    group = 2 * abs(order) - (1 if order > 0 else 0)
    return sum(BLOCK_COUNTS[:group]) + degree - abs(order)


def identity():
    rows = lax.broadcasted_iota(jnp.int32, (CHANNELS, CHANNELS), 0)
    cols = lax.broadcasted_iota(jnp.int32, (CHANNELS, CHANNELS), 1)
    return jnp.where(rows == cols, 1.0, 0.0).astype(jnp.bfloat16)


def mix_kernel(offset, other_offset, place_ref, mixture_ref, own_ref, other_ref, *refs):
    (both, across, here), (own, other, sems) = refs[:3], refs[3:]
    per_group, rows, width = own.shape
    outs = (both.at[:rows], both.at[rows:], across, here)
    blocks = sems.shape[1]
    block = rows // blocks
    copies = []
    for b in range(blocks):
        span = pl.ds(b * block, block)
        source = pl.ds(offset + b * block, block)
        copies.append(
            (
                pltpu.make_async_copy(own_ref.at[:, source, :], own.at[:, span, :], sems.at[0, b]),
                pltpu.make_async_copy(
                    other_ref.at[:, pl.ds(other_offset + b * block, block), :],
                    other.at[:, span, :],
                    sems.at[1, b],
                ),
            )
        )
    for pair in copies:
        for copy in pair:
            copy.start()
    dp = place_ref[0]
    z = dp // 2
    core = dp % 2
    beside = z + 1 - 2 * (z % 2)
    dests = (beside, 3 - beside, 3 - z, z)
    partner = dp + 1 - 2 * core
    coefs = []
    for dest in dests:
        system = 2 * dest + core
        coefs.append(
            [mixture_ref[system, dp * per_group + e] for e in range(per_group)]
            + [mixture_ref[system, partner * per_group + e] for e in range(per_group)]
        )

    def body(step, carry):
        row = pl.multiple_of(step * 16, 16)
        for column in range(0, width, CHANNELS):
            span = pl.ds(column, CHANNELS)
            parts = [own[e, pl.ds(row, 16), span].astype(jnp.float32) for e in range(per_group)]
            parts += [other[e, pl.ds(row, 16), span].astype(jnp.float32) for e in range(per_group)]
            for out, coef in zip(outs, coefs):
                total = coef[0] * parts[0]
                for c, part in zip(coef[1:], parts[1:]):
                    total = total + c * part
                out[pl.ds(row, 16), span] = total.astype(jnp.bfloat16)
        return carry

    for b, pair in enumerate(copies):
        for copy in pair:
            copy.wait()
        lax.fori_loop(b * block // 16, (b + 1) * block // 16, body, 0)


def mix(place, mixture, own, other, offset, other_offset, rows):
    per_group, _, width = other.shape
    blocks = 2 if rows % 32 == 0 else 1
    pair = jax.ShapeDtypeStruct((2 * rows, width), jnp.bfloat16)
    single = jax.ShapeDtypeStruct((rows, width), jnp.bfloat16)
    return pl.pallas_call(
        functools.partial(mix_kernel, offset, other_offset),
        in_specs=[SMEM, SMEM, HBM, ANY],
        out_specs=[VMEM] * 3,
        out_shape=[pair, single, single],
        scratch_shapes=[
            pltpu.VMEM((per_group, rows, width), jnp.bfloat16),
            pltpu.VMEM((per_group, rows, width), jnp.bfloat16),
            pltpu.SemaphoreType.DMA((2, blocks)),
        ],
        compiler_params=PARAMS,
        name="mix",
    )(place, mixture, pltpu.with_memory_space_constraint(own, pltpu.HBM), other)


def pick_kernel(index_ref, features_ref, next_ref, prev_ref):
    own = features_ref.shape[0]
    ghosts = index_ref.shape[2]
    columns = lax.broadcasted_iota(jnp.int32, (ghosts, own), 1)
    for place, out in ((0, next_ref), (1, prev_ref)):
        rows = lax.broadcasted_iota(jnp.int32, (ghosts, own), 0)
        wanted = jnp.zeros((ghosts, own), jnp.int32)
        for g in range(ghosts):
            wanted = jnp.where(rows == g, index_ref[0, place, g], wanted)
        hot = jnp.where(columns == wanted, 1.0, 0.0).astype(jnp.bfloat16)
        out[...] = dot(hot, features_ref[...]).astype(jnp.bfloat16)


def pick_ghosts(index, features):
    out = jax.ShapeDtypeStruct((index.shape[2], features.shape[1]), jnp.bfloat16)
    return pl.pallas_call(
        pick_kernel,
        in_specs=[SMEM, VMEM],
        out_specs=[VMEM] * 2,
        out_shape=[out, out],
        compiler_params=PARAMS,
        name="pick_ghosts",
    )(index, features)


def hot_rows(index, count, values=1.0, start=0):
    rows = lax.broadcasted_iota(jnp.int32, (count, index.shape[1]), 0) + start
    return jnp.where(index == rows, values, 0.0).astype(jnp.bfloat16)


def turn_into(wide, sources, targets):
    step_rows = 32

    def body(step, carry):
        base = pl.multiple_of(step * step_rows, step_rows)
        for degree in range(LMAX + 1):
            extent = 2 * degree + 1
            kept = min(degree, MMAX)
            for order in range(-kept, kept + 1):
                start = degree_start(degree) + extent * (degree + order)
                totals = [0.0] * len(sources)
                for n in range(extent):
                    row = pl.ds((degree * degree + n) * CHANNELS + base, step_rows)
                    factor = wide[pl.ds(start + n, 1), :]
                    totals = [t + factor * s[row, :] for t, s in zip(totals, sources)]
                place = pl.ds(frame_block(degree, order) * CHANNELS + base, step_rows)
                for target, total in zip(targets, totals):
                    target[place, :] = total.astype(jnp.bfloat16)
        return carry

    lax.fori_loop(0, CHANNELS // step_rows, body, 0)


BAND = 16


def packed_rows(own, wigner_rows):
    rotations = COEFFS * own
    targets = rotations + BAND * -(-wigner_rows // BAND)
    return rotations, targets, targets + BAND


def live_targets(count_ref, targets_ref):
    targets = targets_ref[...]
    live = lax.broadcasted_iota(jnp.int32, targets.shape, 1) < count_ref[0, 0]
    return jnp.where(live, targets, -1)


def pack_kernel(count_ref, grad_ref, targets_ref, wigner_ref, out_ref):
    own = grad_ref.shape[0]
    wig_rows, edges = wigner_ref.shape
    rotations_at, targets_at, end = packed_rows(own, wig_rows)
    for n in range(COEFFS):
        out_ref[n * own : (n + 1) * own, :] = grad_ref[:, n * CHANNELS : (n + 1) * CHANNELS]
    padding = jnp.zeros((targets_at - rotations_at - wig_rows, edges), jnp.float32)
    rotations = jnp.concatenate([wigner_ref[...].astype(jnp.float32), padding], 0)
    out_ref[rotations_at:targets_at, :] = rotations.astype(jnp.bfloat16)
    marks = live_targets(count_ref, targets_ref).astype(jnp.float32)
    out_ref[targets_at:end, :] = jnp.broadcast_to(marks, (BAND, edges)).astype(jnp.bfloat16)


def pack_inputs(count, grad_out, targets, wigner):
    rows = packed_rows(grad_out.shape[0], wigner.shape[0])[-1]
    return pl.pallas_call(
        pack_kernel,
        in_specs=[SMEM] + [VMEM] * 3,
        out_specs=VMEM,
        out_shape=jax.ShapeDtypeStruct((rows, wigner.shape[1]), jnp.bfloat16),
        compiler_params=PARAMS,
        name="pack_inputs",
    )(count, grad_out, targets, wigner)


def enter_kernel(
    place_ref, count_ref, features_ref, ghosts_ref, grad_ref, sources_ref, targets_ref, wigner_ref,
    frame_ref, back_ref, *rest,
):
    slabs, (wide, forward, backward, turned, turned_back) = rest[:-5], rest[-5:]
    own = features_ref.shape[0]
    extra = ghosts_ref.shape[0]
    wide[...] = wigner_ref[...].astype(jnp.float32)
    sources = sources_ref[...]
    targets = live_targets(count_ref, targets_ref)
    from_own = hot_rows(sources, own)
    from_ghost = hot_rows(sources, extra, start=own)
    to_own = hot_rows(targets, own, MESSAGE_SCALE)
    for n in range(COEFFS):
        span = pl.ds(n * CHANNELS, CHANNELS)
        forward[span, :] = dot(features_ref[:, span], from_own, TN) + dot(
            ghosts_ref[:, span], from_ghost, TN
        )
        backward[span, :] = dot(grad_ref[:, span], to_own, TN)
    turn_into(wide, (forward, backward), (turned, turned_back))
    eye = identity()
    for k in range(FRAME_BLOCKS):
        span = pl.ds(k * CHANNELS, CHANNELS)
        frame_ref[:, span] = dot(eye, turned[span, :], NT).astype(jnp.bfloat16)
        back_ref[:, span] = dot(eye, turned_back[span, :], NT).astype(jnp.bfloat16)
    spaces = len(slabs)
    for peer, slab in enumerate(slabs):
        position = lax.bitwise_xor(place_ref[1], jnp.int32(peer))
        at = first = 0
        for blocks in BLOCK_COUNTS:
            rows = blocks * CHANNELS // spaces
            begin = pl.multiple_of(first + position * rows, BAND)
            slab[at : at + rows, :] = turned[pl.ds(begin, rows), :]
            at += rows
            first += blocks * CHANNELS


def enter(place, count, features, ghosts, grad_out, sources, targets, wigner, spaces):
    edges = sources.shape[1]
    frame = jax.ShapeDtypeStruct((edges, FRAME_W), jnp.bfloat16)
    slab = jax.ShapeDtypeStruct((FRAME_W // spaces, edges), jnp.bfloat16)
    return pl.pallas_call(
        enter_kernel,
        in_specs=[SMEM, SMEM] + [VMEM] * 6,
        out_specs=[VMEM] * (2 + spaces),
        out_shape=[frame, frame] + [slab] * spaces,
        scratch_shapes=[
            pltpu.VMEM((wigner.shape[0], edges), jnp.float32),
            pltpu.VMEM((NODE_W, edges), jnp.float32),
            pltpu.VMEM((NODE_W, edges), jnp.float32),
            pltpu.VMEM((FRAME_W, edges), jnp.bfloat16),
            pltpu.VMEM((FRAME_W, edges), jnp.bfloat16),
        ],
        compiler_params=PARAMS,
        name="enter_frame",
    )(place, count, features, ghosts, grad_out, sources, targets, wigner)


def peer_frames_kernel(own, wig_rows, *refs):
    packs, (out, wide, backward, turned_back) = refs[:-4], refs[-4:]
    rotations_at, targets_at, end = packed_rows(own, wig_rows)
    eye = identity()
    for peer, pack in enumerate(packs):
        wide[...] = pack[rotations_at:targets_at, :].astype(jnp.float32)
        targets = pack[targets_at:end, :].astype(jnp.float32)[:1].astype(jnp.int32)
        to_own = hot_rows(targets, own, MESSAGE_SCALE)
        for n in range(COEFFS):
            backward[n * CHANNELS : (n + 1) * CHANNELS, :] = dot(
                pack[n * own : (n + 1) * own, :], to_own, TN
            )
        turn_into(wide, (backward,), (turned_back,))
        for k in range(FRAME_BLOCKS):
            span = pl.ds(k * CHANNELS, CHANNELS)
            out[peer, :, span] = dot(eye, turned_back[span, :], NT).astype(jnp.bfloat16)


def peer_frames(packs, own, wig_rows):
    edges = packs[0].shape[1]
    return pl.pallas_call(
        functools.partial(peer_frames_kernel, own, wig_rows),
        in_specs=[VMEM] * len(packs),
        out_specs=VMEM,
        out_shape=jax.ShapeDtypeStruct((len(packs), edges, FRAME_W), jnp.bfloat16),
        scratch_shapes=[
            pltpu.VMEM((BAND * -(-wig_rows // BAND), edges), jnp.float32),
            pltpu.VMEM((NODE_W, edges), jnp.float32),
            pltpu.VMEM((FRAME_W, edges), jnp.bfloat16),
        ],
        compiler_params=PARAMS,
        name="peer_frames",
    )(*packs)


def weight_grad_kernel(scale, back_ref, backs, *refs):
    all_slabs, (out_zero, out_one, out_two) = refs[:-3], refs[-3:]
    spaces = len(all_slabs)
    all_backs = [back_ref] + [backs.at[k] for k in range(spaces - 1)]
    rows = [blocks * CHANNELS // spaces for blocks in BLOCK_COUNTS]
    widths = [blocks * CHANNELS for blocks in BLOCK_COUNTS]

    def product(a, b):
        left = slice(sum(rows[:a]), sum(rows[: a + 1]))
        right = slice(sum(widths[:b]), sum(widths[: b + 1]))
        return sum(dot(s[left, :], d[:, right]) for s, d in zip(all_slabs, all_backs))

    out_zero[...] = (scale * product(0, 0)).astype(jnp.bfloat16)
    for out, group in ((out_one, 1), (out_two, 3)):
        out[0] = (scale * (product(group, group) + product(group + 1, group + 1))).astype(jnp.bfloat16)
        out[1] = (scale * (product(group, group + 1) - product(group + 1, group))).astype(jnp.bfloat16)


def weight_grads(back, backs, slabs, scale):
    spaces = len(slabs)
    k0, k1, _, k2, _ = [blocks * CHANNELS for blocks in BLOCK_COUNTS]
    return pl.pallas_call(
        functools.partial(weight_grad_kernel, scale),
        in_specs=[VMEM] * (2 + spaces),
        out_specs=[VMEM] * 3,
        out_shape=[
            jax.ShapeDtypeStruct((k0 // spaces, k0), jnp.bfloat16),
            jax.ShapeDtypeStruct((2, k1 // spaces, k1), jnp.bfloat16),
            jax.ShapeDtypeStruct((2, k2 // spaces, k2), jnp.bfloat16),
        ],
        compiler_params=PARAMS,
        name="weight_grads",
    )(back, backs, *slabs)


def apply_kernel(group, places, local_rows, place_ref, frame_ref, back_ref, *refs):
    shards, (out_ref, grad_ref, full) = refs[:-3], refs[-3:]
    parts = 1 if group == 0 else 2
    for (peer, first_part, count, offset, rows, at), shard in zip(places, shards):
        position = lax.bitwise_xor(place_ref[1], jnp.int32(peer))
        begin = pl.multiple_of(position * local_rows + offset, 16)
        for k in range(count):
            if at is None:
                full[first_part + k, pl.ds(begin, rows), :] = shard[k * rows : (k + 1) * rows, :]
                continue
            for column in range(BLOCK_COUNTS[group]):
                full[
                    first_part + k,
                    pl.ds(begin, rows),
                    column * CHANNELS : (column + 1) * CHANNELS,
                ] = shard[at : at + rows, :]
                at += rows
    first = sum(BLOCK_COUNTS[:group]) * CHANNELS
    width = BLOCK_COUNTS[group] * CHANNELS
    eye = identity()
    edges = frame_ref.shape[0]

    def put_turned(value, offset):
        value = value.astype(jnp.bfloat16)
        for k in range(0, width, CHANNELS):
            out_ref[offset + k : offset + k + CHANNELS, :] = dot(
                eye, value[:, k : k + CHANNELS], NT
            ).astype(jnp.bfloat16)

    if parts == 1:
        grad_ref[...] = dot(full[0], back_ref[:, first : first + width], NT).astype(jnp.bfloat16)
        put_turned(dot(frame_ref[:, first : first + width], full[0]), 0)
        return
    second = first + width
    back = jnp.concatenate([back_ref[:, first:second], back_ref[:, second : second + width]], 0)
    real = dot(full[0], back, NT)
    imag = dot(full[1], back, NT)
    grad_ref[:width, :] = (real[:, :edges] + imag[:, edges:]).astype(jnp.bfloat16)
    grad_ref[width:, :] = (real[:, edges:] - imag[:, :edges]).astype(jnp.bfloat16)
    frame = jnp.concatenate([frame_ref[:, first:second], frame_ref[:, second : second + width]], 0)
    real = dot(frame, full[0])
    imag = dot(frame, full[1])
    put_turned(real[:edges] - imag[edges:], 0)
    put_turned(imag[:edges] + real[edges:], width)


def apply_weights(group, place, frame, back, pieces, spaces):
    places, shards = zip(*pieces)
    edges = frame.shape[0]
    width = BLOCK_COUNTS[group] * CHANNELS
    parts = 1 if group == 0 else 2
    out = jax.ShapeDtypeStruct((parts * width, edges), jnp.bfloat16)
    return pl.pallas_call(
        functools.partial(apply_kernel, group, places, width // spaces),
        in_specs=[SMEM] + [VMEM] * (2 + len(shards)),
        out_specs=[VMEM] * 2,
        out_shape=[out, out],
        scratch_shapes=[pltpu.VMEM((parts, width, width), jnp.bfloat16)],
        compiler_params=PARAMS,
        name=f"apply_weights_{group}",
    )(place, frame, back, *shards)


def finish_kernel(*refs):
    out = refs[-1]
    at = 0
    for here, beside, opposite in zip(refs[:-1:3], refs[1:-1:3], refs[2:-1:3]):
        rows, width = here.shape
        step = rows if rows < 160 else rows // 2
        for first in range(0, rows, step):
            span = slice(first, first + step)
            for column in range(0, width, CHANNELS):
                lanes = slice(column, column + CHANNELS)
                total = sum(r[span, lanes].astype(jnp.float32) for r in (here, beside, opposite))
                out[at : at + step, :] = total.astype(jnp.bfloat16)
                at += step


def finish(*chunks):
    arrays = [array for chunk in chunks for array in chunk]
    rows = sum(here.size // CHANNELS for here, _, _ in chunks)
    return pl.pallas_call(
        finish_kernel,
        in_specs=[VMEM] * len(arrays),
        out_specs=VMEM,
        out_shape=jax.ShapeDtypeStruct((rows, CHANNELS), jnp.bfloat16),
        compiler_params=PARAMS,
        name="finish_first",
    )(*arrays)


def leave(frames, wigner_ref, wide, turned):
    wide[...] = wigner_ref[...].astype(jnp.float32)
    step_rows = 32

    def body(step, carry):
        base = pl.multiple_of(step * step_rows, step_rows)
        for degree in range(LMAX + 1):
            extent = 2 * degree + 1
            kept = min(degree, MMAX)
            values = []
            for order in range(-kept, kept + 1):
                source = frames[abs(order)]
                block = degree - abs(order)
                if order < 0:
                    block += BLOCK_COUNTS[2 * -order]
                values.append(
                    source[pl.ds(block * CHANNELS + base, step_rows), :].astype(jnp.float32)
                )
            for n in range(extent):
                total = 0.0
                for order, value in zip(range(-kept, kept + 1), values):
                    start = degree_start(degree) + extent * (degree + order) + n
                    total = total + wide[pl.ds(start, 1), :] * value
                row = pl.ds((degree * degree + n) * CHANNELS + base, step_rows)
                turned[row, :] = total.astype(jnp.bfloat16)
        return carry

    lax.fori_loop(0, CHANNELS // step_rows, body, 0)


def leave_back_kernel(
    zero_ref, one_ref, two_ref, wigner_ref, sources_ref, grad_ref, base_ref, ghost_ref, wide, turned
):
    leave((zero_ref, one_ref, two_ref), wigner_ref, wide, turned)
    own = grad_ref.shape[0]
    extra = ghost_ref.shape[0]
    edges = sources_ref.shape[1]
    rows = lax.broadcasted_iota(jnp.int32, (own + extra, edges), 0)
    hot = jnp.where(sources_ref[...] == rows, 1.0, 0.0).astype(jnp.bfloat16)
    for n in range(COEFFS):
        span = pl.ds(n * CHANNELS, CHANNELS)
        table = dot(hot, turned[span, :], NT)
        base_ref[:, span] = grad_ref[:, span].astype(jnp.float32) + table[:own]
        ghost_ref[:, span] = table[own:].astype(jnp.bfloat16)


def leave_kernel(
    zero_ref, one_ref, two_ref, wigner_ref, count_ref, targets_ref, features_ref, out_ref, wide, turned
):
    leave((zero_ref, one_ref, two_ref), wigner_ref, wide, turned)
    own = features_ref.shape[0]
    edges = targets_ref.shape[1]
    rows = lax.broadcasted_iota(jnp.int32, (own, edges), 0)
    live = lax.broadcasted_iota(jnp.int32, (own, edges), 1) < count_ref[0, 0]
    hot = jnp.where((targets_ref[...] == rows) & live, MESSAGE_SCALE, 0.0).astype(jnp.bfloat16)
    for n in range(COEFFS):
        span = pl.ds(n * CHANNELS, CHANNELS)
        out_ref[:, span] = (
            features_ref[:, span].astype(jnp.float32) + dot(hot, turned[span, :], NT)
        ).astype(jnp.bfloat16)


def leave_scratch(wigner):
    rows, edges = wigner.shape
    return [pltpu.VMEM((rows, edges), jnp.float32), pltpu.VMEM((NODE_W, edges), jnp.bfloat16)]


def leave_back(frames, wigner, sources, grad_out, extra):
    own = grad_out.shape[0]
    return pl.pallas_call(
        leave_back_kernel,
        in_specs=[VMEM] * 6,
        out_specs=[VMEM] * 2,
        out_shape=[
            jax.ShapeDtypeStruct((own, NODE_W), jnp.float32),
            jax.ShapeDtypeStruct((extra, NODE_W), jnp.bfloat16),
        ],
        scratch_shapes=leave_scratch(wigner),
        compiler_params=PARAMS,
        name="leave_frame_back",
    )(*frames, wigner, sources, grad_out)


def leave_forward(frames, wigner, count, targets, features):
    return pl.pallas_call(
        leave_kernel,
        in_specs=[VMEM] * 4 + [SMEM] + [VMEM] * 2,
        out_specs=VMEM,
        out_shape=jax.ShapeDtypeStruct(features.shape, jnp.bfloat16),
        scratch_shapes=leave_scratch(wigner),
        compiler_params=PARAMS,
        name="leave_frame",
    )(*frames, wigner, count, targets, features)


def settle_kernel(base_ref, next_ref, prev_ref, index_ref, out_ref):
    own = base_ref.shape[0]
    ghosts = next_ref.shape[0]
    rows = lax.broadcasted_iota(jnp.int32, (own, ghosts), 0)
    total = base_ref[...]
    for place, ref in ((0, next_ref), (1, prev_ref)):
        hot = jnp.where(index_ref[place : place + 1, :] == rows, 1.0, 0.0)
        total = total + dot(hot, ref[...].astype(jnp.float32))
    out_ref[...] = total.astype(jnp.bfloat16)


def settle(base, from_next, from_prev, index):
    return pl.pallas_call(
        settle_kernel,
        in_specs=[VMEM] * 4,
        out_specs=VMEM,
        out_shape=jax.ShapeDtypeStruct(base.shape, jnp.bfloat16),
        compiler_params=PARAMS,
        name="settle_ghosts",
    )(base, from_next, from_prev, index)


def together(*values):
    return lax.optimization_barrier(values)


CORES = [(i, i ^ 1) for i in range(8)]
BESIDE = [(2 * z + c, 2 * (z ^ 1) + c) for z in range(4) for c in range(2)]
OPPOSITE = [(2 * z + c, 2 * (3 - z) + c) for z in range(4) for c in range(2)]


def add(*parts):
    return sum(part.astype(jnp.float32) for part in parts).astype(jnp.bfloat16)


def mixed_general(mixture, own):
    per_group = own.shape[0]
    columns = lax.dynamic_slice_in_dim(mixture, lax.axis_index("dp") * per_group, per_group, 1)
    sums = jnp.einsum(
        "se,erk->srk", columns, own.astype(jnp.float32), precision=lax.Precision.HIGHEST
    ).astype(jnp.bfloat16)
    return lax.psum_scatter(sums, "dp", scatter_dimension=0, tiled=False)


def to_peer(array, spaces, k):
    return lax.ppermute(array, "space", [(i, i ^ k) for i in range(spaces)])


def on_device(
    features,
    grad_out,
    wigner,
    sources,
    targets,
    ghost_index,
    edge_count,
    mixture,
    w_zero,
    w_one,
    w_two,
):
    edges = sources.shape[0]
    own_rows = features.shape[0]
    ghosts = ghost_index.shape[2]
    spaces = lax.axis_size("space")
    place = jnp.stack([lax.axis_index("dp"), lax.axis_index("space")]).astype(jnp.int32)
    up = [(i, (i + 1) % spaces) for i in range(spaces)]
    down = [(j, i) for i, j in up]
    per_group, rows_zero = w_zero.shape[:2]
    rows_one, rows_two = w_one.shape[2], w_two.shape[2]
    sources = sources.reshape(1, edges)
    targets = targets.reshape(1, edges)
    w_one = w_one.reshape(per_group, -1, w_one.shape[-1])
    w_two = w_two.reshape(per_group, -1, w_two.shape[-1])
    scale = float(edges * spaces) ** (-0.5)

    def frames(from_prev, from_next):
        return enter(
            place,
            edge_count,
            features,
            jnp.concatenate([from_prev, from_next], 0),
            grad_out,
            sources,
            targets,
            wigner,
            spaces,
        )

    to_next, to_prev = pick_ghosts(ghost_index, features)

    if lax.axis_size("dp") == 8 and spaces == 4:
        half = rows_zero // 2
        chunks = [
            (0, w_zero, 0, half, (0, 1, 0)),
            (3, w_two, 0, 2 * rows_two, (0, 2, 0)),
            (1, w_one, 0, rows_one, (0, 1, 0)),
            (1, w_one, rows_one, rows_one, (1, 1, 0)),
            (0, w_zero, half, rows_zero - half, (0, 1, half)),
        ]

        def swap_cores(array):
            return lax.ppermute(array, "dp", CORES)

        def mix_chunk(j, other, other_first=0):
            _, own, first, rows, _ = chunks[j]
            return mix(place, mixture, own, other, first, other_first, rows)

        def swap_beside(both):
            return lax.ppermute(both, "dp", BESIDE)

        def total_opposite(j, across, beside):
            return add(across, beside[chunks[j][3] :])

        def swap_opposite(total):
            return lax.ppermute(total, "dp", OPPOSITE)

        def total_here(j, here, beside, opposite):
            return add(here, beside[: chunks[j][3]], opposite)

        def to_sides(shard):
            return to_peer(shard, spaces, 1), to_peer(shard, spaces, 2)

        def forward(j, sides):
            along = 1 if j == 1 else 2
            return to_peer(sides[(3 ^ along) - 1], spaces, along)

        def pieces(j, shard, sides, last, at=None):
            _, _, _, rows, (part, parts, offset) = chunks[j]
            return [
                ((k, part, parts, offset, rows // parts, at), a)
                for k, a in enumerate((shard, *sides, last))
            ]

        other0 = swap_cores(w_zero)
        other0, to_next, to_prev = together(other0, to_next, to_prev)
        both0, across0, here0 = mix_chunk(0, other0)
        beside0 = swap_beside(both0)
        from_prev = lax.ppermute(to_next, "space", up)
        from_next = lax.ppermute(to_prev, "space", down)
        sent, other0 = together(w_two, other0)
        other1 = swap_cores(sent)
        raw = pack_inputs(edge_count, grad_out, targets, wigner)
        raws = [to_peer(raw, spaces, 1), to_peer(raw, spaces, 2)]
        both1, across1, here1 = mix_chunk(1, other1)
        beside1 = swap_beside(both1)
        beside0, here1, from_prev, from_next = together(beside0, here1, from_prev, from_next)
        total0 = total_opposite(0, across0, beside0)
        opposite0 = swap_opposite(total0)
        sent, other1, here1 = together(w_one, other1, here1)
        other2 = swap_cores(sent)
        total0, from_prev, from_next = together(total0, from_prev, from_next)
        frame, back, *slabs = frames(from_prev, from_next)
        slabs[1], slabs[2], other2 = together(slabs[1], slabs[2], other2)
        slabs[1], slabs[2] = to_peer(slabs[1], spaces, 1), to_peer(slabs[2], spaces, 2)
        raw, frame, *raws = together(raw, frame, *raws)
        raws.append(to_peer(raw, spaces, 3))
        other2, frame = together(other2, frame)
        both2, across2, here2 = mix_chunk(2, other2)
        both3, across3, here3 = mix_chunk(3, other2, rows_one)
        both2, here2, here3, opposite0 = together(both2, here2, here3, opposite0)
        beside2 = swap_beside(both2)
        here3, raws[2] = together(here3, raws[2])
        backs = peer_frames(raws, own_rows, wigner.shape[0])
        beside1, here2, here3, backs = together(beside1, here2, here3, backs)
        total1 = total_opposite(1, across1, beside1)
        opposite1 = swap_opposite(total1)
        other0, beside1 = together(other0, beside1)
        both4, across4, here4 = mix_chunk(4, other0, half)
        both3, beside2, here4 = together(both3, beside2, here4)
        beside3 = swap_beside(both3)
        total2 = total_opposite(2, across2, beside2)
        opposite2 = swap_opposite(total2)
        beside2, *slabs[1:] = together(beside2, *slabs[1:])
        slabs[3] = to_peer(slabs[3], spaces, 3)
        opposite1, beside2 = together(opposite1, beside2)
        shard1 = finish((here0, beside0, opposite0), (here1, beside1, opposite1))
        sides1 = to_sides(shard1)
        both4, beside3, shard1 = together(both4, beside3, shard1)
        beside4 = swap_beside(both4)
        total3 = total_opposite(3, across3, beside3)
        opposite3 = swap_opposite(total3)
        shard2 = total_here(2, here2, beside2, opposite2)
        shard2, *sides1 = together(shard2, *sides1)
        forward1 = forward(1, sides1)
        sides2 = to_sides(shard2)
        beside4, shard2, slabs[3] = together(beside4, shard2, slabs[3])
        total4 = total_opposite(4, across4, beside4)
        opposite4 = swap_opposite(total4)
        opposite3, total4 = together(opposite3, total4)
        shard3 = total_here(3, here3, beside3, opposite3)
        sides3 = to_sides(shard3)
        opposite4, *sides2 = together(opposite4, *sides2)
        shard4 = total_here(4, here4, beside4, opposite4)
        late_back, shard4, slabs[3] = together(back, shard4, slabs[3])
        grad_mix = weight_grads(late_back, backs, slabs, scale)
        sides4 = to_sides(shard4)
        forward2 = forward(2, sides2)
        shard4 = total_here(4, here4, beside4, opposite4)
        late_back, shard4, slabs[3] = together(back, shard4, slabs[3])
        grad_mix = weight_grads(late_back, backs, slabs, scale)
        sides4 = to_sides(shard4)
        outs, grads = {}, {}
        whole = {
            3: pieces(1, shard1, sides1, forward1, half * BLOCK_COUNTS[0]),
            1: pieces(2, shard2, sides2, forward2) + pieces(3, shard3, sides3, forward(3, sides3)),
            0: pieces(0, shard1, sides1, forward1, 0) + pieces(4, shard4, sides4, to_peer(shard4, spaces, 3)),
        }
    else:
        from_prev = lax.ppermute(to_next, "space", up)
        from_next = lax.ppermute(to_prev, "space", down)
        frame, back, *slabs = frames(from_prev, from_next)
        slabs = [slabs[0]] + [to_peer(slabs[k], spaces, k) for k in range(1, spaces)]
        raw = pack_inputs(edge_count, grad_out, targets, wigner)
        raws = [to_peer(raw, spaces, k) for k in range(1, spaces)]
        backs = peer_frames(raws, own_rows, wigner.shape[0])
        grad_mix = weight_grads(back, backs, slabs, scale)
        outs, grads, whole = {}, {}, {}
        for group, own, parts in ((3, w_two, 2), (1, w_one, 2), (0, w_zero, 1)):
            shard = mixed_general(mixture, own)
            rows = shard.shape[0] // parts

            def place_of(k):
                return (k, 0, parts, 0, rows, None)

            whole[group] = [(place_of(0), shard)] + [
                (place_of(k), to_peer(shard, spaces, k)) for k in range(1, spaces)
            ]

    for group, pieces_of in whole.items():
        if group == 0:
            frame, grads[1], *grad_mix = together(frame, grads[1], *grad_mix)
        outs[group], grads[group] = apply_weights(group, place, frame, back, pieces_of, spaces)
    base, returning = leave_back(
        [grads[g] for g in (0, 1, 3)], wigner, sources, grad_out, 2 * ghosts
    )
    back_next = lax.ppermute(returning[:ghosts], "space", down)
    back_prev = lax.ppermute(returning[ghosts:], "space", up)
    updated = leave_forward([outs[g] for g in (0, 1, 3)], wigner, edge_count, targets, features)
    grad_features = settle(base, back_next, back_prev, ghost_index[0])
    grad_mix0, grad_mix1, grad_mix2 = grad_mix
    return (updated, grad_features, grad_mix0[None], grad_mix1[None], grad_mix2[None])


def solution(mesh):
    return jax.shard_map(
        on_device,
        mesh=mesh,
        in_specs=(
            P(("dp", "space"), None),
            P(("dp", "space"), None),
            P(None, ("dp", "space")),
            P(("dp", "space")),
            P(("dp", "space")),
            P(("dp", "space"), None, None),
            P("dp", "space"),
            P(),
            P("dp", "space", None),
            P("dp", None, "space", None),
            P("dp", None, "space", None),
        ),
        out_specs=(
            P(("dp", "space"), None),
            P(("dp", "space"), None),
            P("dp", "space", None),
            P("dp", None, "space", None),
            P("dp", None, "space", None),
        ),
        check_vma=False,
    )
```

```python
import functools

import jax
import jax.numpy as jnp
from jax import lax
from jax.experimental import pallas as pl
from jax.experimental.pallas import tpu as pltpu
from jax.sharding import PartitionSpec as P

CHANNELS = 128
LMAX = 6
MMAX = 2
MESSAGE_SCALE = 0.25

BLOCK_COUNTS = (LMAX + 1, LMAX, LMAX, LMAX - 1, LMAX - 1)
FRAME_BLOCKS = sum(BLOCK_COUNTS)
FRAME_W = FRAME_BLOCKS * CHANNELS
COEFFS = (LMAX + 1) ** 2
NODE_W = COEFFS * CHANNELS

NN = (((1,), (0,)), ((), ()))
NT = (((1,), (1,)), ((), ()))
TN = (((0,), (0,)), ((), ()))

PARAMS = pltpu.CompilerParams(vmem_limit_bytes=48 * 1024 * 1024)
VMEM = pl.BlockSpec(memory_space=pltpu.VMEM)
SMEM = pl.BlockSpec(memory_space=pltpu.SMEM)
ANY = pl.BlockSpec(memory_space=pl.ANY)
HBM = pl.BlockSpec(memory_space=pltpu.HBM)


def dot(a, b, dims=NN):
    return lax.dot_general(a, b, dims, preferred_element_type=jnp.float32)


def degree_start(degree):
    return degree * (2 * degree - 1) * (2 * degree + 1) // 3


def frame_block(degree, order):
    if order == 0:
        return degree
    group = 2 * abs(order) - (1 if order > 0 else 0)
    return sum(BLOCK_COUNTS[:group]) + degree - abs(order)


def identity():
    rows = lax.broadcasted_iota(jnp.int32, (CHANNELS, CHANNELS), 0)
    cols = lax.broadcasted_iota(jnp.int32, (CHANNELS, CHANNELS), 1)
    return jnp.where(rows == cols, 1.0, 0.0).astype(jnp.bfloat16)


def mix_kernel(offset, other_offset, place_ref, mixture_ref, own_ref, other_ref, *refs):
    (both, across, here), (own, other, sems) = refs[:3], refs[3:]
    per_group, rows, width = own.shape
    outs = (both.at[:rows], both.at[rows:], across, here)
    blocks = sems.shape[1]
    block = rows // blocks
    copies = []
    for b in range(blocks):
        span = pl.ds(b * block, block)
        source = pl.ds(offset + b * block, block)
        copies.append(
            (
                pltpu.make_async_copy(own_ref.at[:, source, :], own.at[:, span, :], sems.at[0, b]),
                pltpu.make_async_copy(
                    other_ref.at[:, pl.ds(other_offset + b * block, block), :],
                    other.at[:, span, :],
                    sems.at[1, b],
                ),
            )
        )
    for pair in copies:
        for copy in pair:
            copy.start()
    dp = place_ref[0]
    z = dp // 2
    core = dp % 2
    beside = z + 1 - 2 * (z % 2)
    dests = (beside, 3 - beside, 3 - z, z)
    partner = dp + 1 - 2 * core
    coefs = []
    for dest in dests:
        system = 2 * dest + core
        coefs.append(
            [mixture_ref[system, dp * per_group + e] for e in range(per_group)]
            + [mixture_ref[system, partner * per_group + e] for e in range(per_group)]
        )

    def body(step, carry):
        row = pl.multiple_of(step * 16, 16)
        for column in range(0, width, CHANNELS):
            span = pl.ds(column, CHANNELS)
            parts = [own[e, pl.ds(row, 16), span].astype(jnp.float32) for e in range(per_group)]
            parts += [other[e, pl.ds(row, 16), span].astype(jnp.float32) for e in range(per_group)]
            for out, coef in zip(outs, coefs):
                total = coef[0] * parts[0]
                for c, part in zip(coef[1:], parts[1:]):
                    total = total + c * part
                out[pl.ds(row, 16), span] = total.astype(jnp.bfloat16)
        return carry

    for b, pair in enumerate(copies):
        for copy in pair:
            copy.wait()
        lax.fori_loop(b * block // 16, (b + 1) * block // 16, body, 0)


def mix(place, mixture, own, other, offset, other_offset, rows):
    per_group, _, width = other.shape
    blocks = 2 if rows % 32 == 0 else 1
    pair = jax.ShapeDtypeStruct((2 * rows, width), jnp.bfloat16)
    single = jax.ShapeDtypeStruct((rows, width), jnp.bfloat16)
    return pl.pallas_call(
        functools.partial(mix_kernel, offset, other_offset),
        in_specs=[SMEM, SMEM, HBM, ANY],
        out_specs=[VMEM] * 3,
        out_shape=[pair, single, single],
        scratch_shapes=[
            pltpu.VMEM((per_group, rows, width), jnp.bfloat16),
            pltpu.VMEM((per_group, rows, width), jnp.bfloat16),
            pltpu.SemaphoreType.DMA((2, blocks)),
        ],
        compiler_params=PARAMS,
        name="mix",
    )(place, mixture, pltpu.with_memory_space_constraint(own, pltpu.HBM), other)


def pick_kernel(index_ref, features_ref, next_ref, prev_ref):
    own = features_ref.shape[0]
    ghosts = index_ref.shape[2]
    columns = lax.broadcasted_iota(jnp.int32, (ghosts, own), 1)
    for place, out in ((0, next_ref), (1, prev_ref)):
        rows = lax.broadcasted_iota(jnp.int32, (ghosts, own), 0)
        wanted = jnp.zeros((ghosts, own), jnp.int32)
        for g in range(ghosts):
            wanted = jnp.where(rows == g, index_ref[0, place, g], wanted)
        hot = jnp.where(columns == wanted, 1.0, 0.0).astype(jnp.bfloat16)
        out[...] = dot(hot, features_ref[...]).astype(jnp.bfloat16)


def pick_ghosts(index, features):
    out = jax.ShapeDtypeStruct((index.shape[2], features.shape[1]), jnp.bfloat16)
    return pl.pallas_call(
        pick_kernel,
        in_specs=[SMEM, VMEM],
        out_specs=[VMEM] * 2,
        out_shape=[out, out],
        compiler_params=PARAMS,
        name="pick_ghosts",
    )(index, features)


def hot_rows(index, count, values=1.0, start=0):
    rows = lax.broadcasted_iota(jnp.int32, (count, index.shape[1]), 0) + start
    return jnp.where(index == rows, values, 0.0).astype(jnp.bfloat16)


def turn_into(wide, sources, targets):
    step_rows = 32

    def body(step, carry):
        base = pl.multiple_of(step * step_rows, step_rows)
        for degree in range(LMAX + 1):
            extent = 2 * degree + 1
            kept = min(degree, MMAX)
            for order in range(-kept, kept + 1):
                start = degree_start(degree) + extent * (degree + order)
                totals = [0.0] * len(sources)
                for n in range(extent):
                    row = pl.ds((degree * degree + n) * CHANNELS + base, step_rows)
                    factor = wide[pl.ds(start + n, 1), :]
                    totals = [t + factor * s[row, :] for t, s in zip(totals, sources)]
                place = pl.ds(frame_block(degree, order) * CHANNELS + base, step_rows)
                for target, total in zip(targets, totals):
                    target[place, :] = total.astype(jnp.bfloat16)
        return carry

    lax.fori_loop(0, CHANNELS // step_rows, body, 0)


BAND = 16


def packed_rows(own, wigner_rows):
    rotations = COEFFS * own
    targets = rotations + BAND * -(-wigner_rows // BAND)
    return rotations, targets, targets + BAND


def live_targets(count_ref, targets_ref):
    targets = targets_ref[...]
    live = lax.broadcasted_iota(jnp.int32, targets.shape, 1) < count_ref[0, 0]
    return jnp.where(live, targets, -1)


def pack_kernel(count_ref, grad_ref, targets_ref, wigner_ref, out_ref):
    own = grad_ref.shape[0]
    wig_rows, edges = wigner_ref.shape
    rotations_at, targets_at, end = packed_rows(own, wig_rows)
    for n in range(COEFFS):
        out_ref[n * own : (n + 1) * own, :] = grad_ref[:, n * CHANNELS : (n + 1) * CHANNELS]
    padding = jnp.zeros((targets_at - rotations_at - wig_rows, edges), jnp.float32)
    rotations = jnp.concatenate([wigner_ref[...].astype(jnp.float32), padding], 0)
    out_ref[rotations_at:targets_at, :] = rotations.astype(jnp.bfloat16)
    marks = live_targets(count_ref, targets_ref).astype(jnp.float32)
    out_ref[targets_at:end, :] = jnp.broadcast_to(marks, (BAND, edges)).astype(jnp.bfloat16)


def pack_inputs(count, grad_out, targets, wigner):
    rows = packed_rows(grad_out.shape[0], wigner.shape[0])[-1]
    return pl.pallas_call(
        pack_kernel,
        in_specs=[SMEM] + [VMEM] * 3,
        out_specs=VMEM,
        out_shape=jax.ShapeDtypeStruct((rows, wigner.shape[1]), jnp.bfloat16),
        compiler_params=PARAMS,
        name="pack_inputs",
    )(count, grad_out, targets, wigner)


def enter_kernel(
    place_ref, count_ref, features_ref, ghosts_ref, grad_ref, sources_ref, targets_ref, wigner_ref,
    frame_ref, back_ref, *rest,
):
    slabs, (wide, forward, backward, turned, turned_back) = rest[:-5], rest[-5:]
    own = features_ref.shape[0]
    extra = ghosts_ref.shape[0]
    wide[...] = wigner_ref[...].astype(jnp.float32)
    sources = sources_ref[...]
    targets = live_targets(count_ref, targets_ref)
    from_own = hot_rows(sources, own)
    from_ghost = hot_rows(sources, extra, start=own)
    to_own = hot_rows(targets, own, MESSAGE_SCALE)
    for n in range(COEFFS):
        span = pl.ds(n * CHANNELS, CHANNELS)
        forward[span, :] = dot(features_ref[:, span], from_own, TN) + dot(
            ghosts_ref[:, span], from_ghost, TN
        )
        backward[span, :] = dot(grad_ref[:, span], to_own, TN)
    turn_into(wide, (forward, backward), (turned, turned_back))
    eye = identity()
    for k in range(FRAME_BLOCKS):
        span = pl.ds(k * CHANNELS, CHANNELS)
        frame_ref[:, span] = dot(eye, turned[span, :], NT).astype(jnp.bfloat16)
        back_ref[:, span] = dot(eye, turned_back[span, :], NT).astype(jnp.bfloat16)
    spaces = len(slabs)
    for peer, slab in enumerate(slabs):
        position = lax.bitwise_xor(place_ref[1], jnp.int32(peer))
        at = first = 0
        for blocks in BLOCK_COUNTS:
            rows = blocks * CHANNELS // spaces
            begin = pl.multiple_of(first + position * rows, BAND)
            slab[at : at + rows, :] = turned[pl.ds(begin, rows), :]
            at += rows
            first += blocks * CHANNELS


def enter(place, count, features, ghosts, grad_out, sources, targets, wigner, spaces):
    edges = sources.shape[1]
    frame = jax.ShapeDtypeStruct((edges, FRAME_W), jnp.bfloat16)
    slab = jax.ShapeDtypeStruct((FRAME_W // spaces, edges), jnp.bfloat16)
    return pl.pallas_call(
        enter_kernel,
        in_specs=[SMEM, SMEM] + [VMEM] * 6,
        out_specs=[VMEM] * (2 + spaces),
        out_shape=[frame, frame] + [slab] * spaces,
        scratch_shapes=[
            pltpu.VMEM((wigner.shape[0], edges), jnp.float32),
            pltpu.VMEM((NODE_W, edges), jnp.float32),
            pltpu.VMEM((NODE_W, edges), jnp.float32),
            pltpu.VMEM((FRAME_W, edges), jnp.bfloat16),
            pltpu.VMEM((FRAME_W, edges), jnp.bfloat16),
        ],
        compiler_params=PARAMS,
        name="enter_frame",
    )(place, count, features, ghosts, grad_out, sources, targets, wigner)


def peer_frames_kernel(own, wig_rows, *refs):
    packs, (out, wide, backward, turned_back) = refs[:-4], refs[-4:]
    rotations_at, targets_at, end = packed_rows(own, wig_rows)
    eye = identity()
    for peer, pack in enumerate(packs):
        wide[...] = pack[rotations_at:targets_at, :].astype(jnp.float32)
        targets = pack[targets_at:end, :].astype(jnp.float32)[:1].astype(jnp.int32)
        to_own = hot_rows(targets, own, MESSAGE_SCALE)
        for n in range(COEFFS):
            backward[n * CHANNELS : (n + 1) * CHANNELS, :] = dot(
                pack[n * own : (n + 1) * own, :], to_own, TN
            )
        turn_into(wide, (backward,), (turned_back,))
        for k in range(FRAME_BLOCKS):
            span = pl.ds(k * CHANNELS, CHANNELS)
            out[peer, :, span] = dot(eye, turned_back[span, :], NT).astype(jnp.bfloat16)


def peer_frames(packs, own, wig_rows):
    edges = packs[0].shape[1]
    return pl.pallas_call(
        functools.partial(peer_frames_kernel, own, wig_rows),
        in_specs=[VMEM] * len(packs),
        out_specs=VMEM,
        out_shape=jax.ShapeDtypeStruct((len(packs), edges, FRAME_W), jnp.bfloat16),
        scratch_shapes=[
            pltpu.VMEM((BAND * -(-wig_rows // BAND), edges), jnp.float32),
            pltpu.VMEM((NODE_W, edges), jnp.float32),
            pltpu.VMEM((FRAME_W, edges), jnp.bfloat16),
        ],
        compiler_params=PARAMS,
        name="peer_frames",
    )(*packs)


def weight_grad_kernel(scale, back_ref, backs, *refs):
    all_slabs, (out_zero, out_one, out_two) = refs[:-3], refs[-3:]
    spaces = len(all_slabs)
    all_backs = [back_ref] + [backs.at[k] for k in range(spaces - 1)]
    rows = [blocks * CHANNELS // spaces for blocks in BLOCK_COUNTS]
    widths = [blocks * CHANNELS for blocks in BLOCK_COUNTS]

    def product(a, b):
        left = slice(sum(rows[:a]), sum(rows[: a + 1]))
        right = slice(sum(widths[:b]), sum(widths[: b + 1]))
        return sum(dot(s[left, :], d[:, right]) for s, d in zip(all_slabs, all_backs))

    out_zero[...] = (scale * product(0, 0)).astype(jnp.bfloat16)
    for out, group in ((out_one, 1), (out_two, 3)):
        out[0] = (scale * (product(group, group) + product(group + 1, group + 1))).astype(jnp.bfloat16)
        out[1] = (scale * (product(group, group + 1) - product(group + 1, group))).astype(jnp.bfloat16)


def weight_grads(back, backs, slabs, scale):
    spaces = len(slabs)
    k0, k1, _, k2, _ = [blocks * CHANNELS for blocks in BLOCK_COUNTS]
    return pl.pallas_call(
        functools.partial(weight_grad_kernel, scale),
        in_specs=[VMEM] * (2 + spaces),
        out_specs=[VMEM] * 3,
        out_shape=[
            jax.ShapeDtypeStruct((k0 // spaces, k0), jnp.bfloat16),
            jax.ShapeDtypeStruct((2, k1 // spaces, k1), jnp.bfloat16),
            jax.ShapeDtypeStruct((2, k2 // spaces, k2), jnp.bfloat16),
        ],
        compiler_params=PARAMS,
        name="weight_grads",
    )(back, backs, *slabs)


def apply_kernel(group, places, local_rows, place_ref, frame_ref, back_ref, *refs):
    shards, (out_ref, grad_ref, full) = refs[:-3], refs[-3:]
    parts = 1 if group == 0 else 2
    for (peer, first_part, count, offset, rows, at), shard in zip(places, shards):
        position = lax.bitwise_xor(place_ref[1], jnp.int32(peer))
        begin = pl.multiple_of(position * local_rows + offset, 16)
        for k in range(count):
            if at is None:
                full[first_part + k, pl.ds(begin, rows), :] = shard[k * rows : (k + 1) * rows, :]
                continue
            for column in range(BLOCK_COUNTS[group]):
                full[
                    first_part + k,
                    pl.ds(begin, rows),
                    column * CHANNELS : (column + 1) * CHANNELS,
                ] = shard[at : at + rows, :]
                at += rows
    first = sum(BLOCK_COUNTS[:group]) * CHANNELS
    width = BLOCK_COUNTS[group] * CHANNELS
    eye = identity()
    edges = frame_ref.shape[0]

    def put_turned(value, offset):
        value = value.astype(jnp.bfloat16)
        for k in range(0, width, CHANNELS):
            out_ref[offset + k : offset + k + CHANNELS, :] = dot(
                eye, value[:, k : k + CHANNELS], NT
            ).astype(jnp.bfloat16)

    if parts == 1:
        grad_ref[...] = dot(full[0], back_ref[:, first : first + width], NT).astype(jnp.bfloat16)
        put_turned(dot(frame_ref[:, first : first + width], full[0]), 0)
        return
    second = first + width
    back = jnp.concatenate([back_ref[:, first:second], back_ref[:, second : second + width]], 0)
    real = dot(full[0], back, NT)
    imag = dot(full[1], back, NT)
    grad_ref[:width, :] = (real[:, :edges] + imag[:, edges:]).astype(jnp.bfloat16)
    grad_ref[width:, :] = (real[:, edges:] - imag[:, :edges]).astype(jnp.bfloat16)
    frame = jnp.concatenate([frame_ref[:, first:second], frame_ref[:, second : second + width]], 0)
    real = dot(frame, full[0])
    imag = dot(frame, full[1])
    put_turned(real[:edges] - imag[edges:], 0)
    put_turned(imag[:edges] + real[edges:], width)


def apply_weights(group, place, frame, back, pieces, spaces):
    places, shards = zip(*pieces)
    edges = frame.shape[0]
    width = BLOCK_COUNTS[group] * CHANNELS
    parts = 1 if group == 0 else 2
    out = jax.ShapeDtypeStruct((parts * width, edges), jnp.bfloat16)
    return pl.pallas_call(
        functools.partial(apply_kernel, group, places, width // spaces),
        in_specs=[SMEM] + [VMEM] * (2 + len(shards)),
        out_specs=[VMEM] * 2,
        out_shape=[out, out],
        scratch_shapes=[pltpu.VMEM((parts, width, width), jnp.bfloat16)],
        compiler_params=PARAMS,
        name=f"apply_weights_{group}",
    )(place, frame, back, *shards)


def finish_kernel(*refs):
    out = refs[-1]
    at = 0
    for here, beside, opposite in zip(refs[:-1:3], refs[1:-1:3], refs[2:-1:3]):
        rows, width = here.shape
        step = rows if rows < 160 else rows // 2
        for first in range(0, rows, step):
            span = slice(first, first + step)
            for column in range(0, width, CHANNELS):
                lanes = slice(column, column + CHANNELS)
                total = sum(r[span, lanes].astype(jnp.float32) for r in (here, beside, opposite))
                out[at : at + step, :] = total.astype(jnp.bfloat16)
                at += step


def finish(*chunks):
    arrays = [array for chunk in chunks for array in chunk]
    rows = sum(here.size // CHANNELS for here, _, _ in chunks)
    return pl.pallas_call(
        finish_kernel,
        in_specs=[VMEM] * len(arrays),
        out_specs=VMEM,
        out_shape=jax.ShapeDtypeStruct((rows, CHANNELS), jnp.bfloat16),
        compiler_params=PARAMS,
        name="finish_first",
    )(*arrays)


def leave(frames, wigner_ref, wide, turned):
    wide[...] = wigner_ref[...].astype(jnp.float32)
    step_rows = 32

    def body(step, carry):
        base = pl.multiple_of(step * step_rows, step_rows)
        for degree in range(LMAX + 1):
            extent = 2 * degree + 1
            kept = min(degree, MMAX)
            values = []
            for order in range(-kept, kept + 1):
                source = frames[abs(order)]
                block = degree - abs(order)
                if order < 0:
                    block += BLOCK_COUNTS[2 * -order]
                values.append(
                    source[pl.ds(block * CHANNELS + base, step_rows), :].astype(jnp.float32)
                )
            for n in range(extent):
                total = 0.0
                for order, value in zip(range(-kept, kept + 1), values):
                    start = degree_start(degree) + extent * (degree + order) + n
                    total = total + wide[pl.ds(start, 1), :] * value
                row = pl.ds((degree * degree + n) * CHANNELS + base, step_rows)
                turned[row, :] = total.astype(jnp.bfloat16)
        return carry

    lax.fori_loop(0, CHANNELS // step_rows, body, 0)


def leave_back_kernel(
    zero_ref, one_ref, two_ref, wigner_ref, sources_ref, grad_ref, base_ref, ghost_ref, wide, turned
):
    leave((zero_ref, one_ref, two_ref), wigner_ref, wide, turned)
    own = grad_ref.shape[0]
    extra = ghost_ref.shape[0]
    edges = sources_ref.shape[1]
    rows = lax.broadcasted_iota(jnp.int32, (own + extra, edges), 0)
    hot = jnp.where(sources_ref[...] == rows, 1.0, 0.0).astype(jnp.bfloat16)
    for n in range(COEFFS):
        span = pl.ds(n * CHANNELS, CHANNELS)
        table = dot(hot, turned[span, :], NT)
        base_ref[:, span] = grad_ref[:, span].astype(jnp.float32) + table[:own]
        ghost_ref[:, span] = table[own:].astype(jnp.bfloat16)


def leave_kernel(
    zero_ref, one_ref, two_ref, wigner_ref, count_ref, targets_ref, features_ref, out_ref, wide, turned
):
    leave((zero_ref, one_ref, two_ref), wigner_ref, wide, turned)
    own = features_ref.shape[0]
    edges = targets_ref.shape[1]
    rows = lax.broadcasted_iota(jnp.int32, (own, edges), 0)
    live = lax.broadcasted_iota(jnp.int32, (own, edges), 1) < count_ref[0, 0]
    hot = jnp.where((targets_ref[...] == rows) & live, MESSAGE_SCALE, 0.0).astype(jnp.bfloat16)
    for n in range(COEFFS):
        span = pl.ds(n * CHANNELS, CHANNELS)
        out_ref[:, span] = (
            features_ref[:, span].astype(jnp.float32) + dot(hot, turned[span, :], NT)
        ).astype(jnp.bfloat16)


def leave_scratch(wigner):
    rows, edges = wigner.shape
    return [pltpu.VMEM((rows, edges), jnp.float32), pltpu.VMEM((NODE_W, edges), jnp.bfloat16)]


def leave_back(frames, wigner, sources, grad_out, extra):
    own = grad_out.shape[0]
    return pl.pallas_call(
        leave_back_kernel,
        in_specs=[VMEM] * 6,
        out_specs=[VMEM] * 2,
        out_shape=[
            jax.ShapeDtypeStruct((own, NODE_W), jnp.float32),
            jax.ShapeDtypeStruct((extra, NODE_W), jnp.bfloat16),
        ],
        scratch_shapes=leave_scratch(wigner),
        compiler_params=PARAMS,
        name="leave_frame_back",
    )(*frames, wigner, sources, grad_out)


def leave_forward(frames, wigner, count, targets, features):
    return pl.pallas_call(
        leave_kernel,
        in_specs=[VMEM] * 4 + [SMEM] + [VMEM] * 2,
        out_specs=VMEM,
        out_shape=jax.ShapeDtypeStruct(features.shape, jnp.bfloat16),
        scratch_shapes=leave_scratch(wigner),
        compiler_params=PARAMS,
        name="leave_frame",
    )(*frames, wigner, count, targets, features)


def settle_kernel(base_ref, next_ref, prev_ref, index_ref, out_ref):
    own = base_ref.shape[0]
    ghosts = next_ref.shape[0]
    rows = lax.broadcasted_iota(jnp.int32, (own, ghosts), 0)
    total = base_ref[...]
    for place, ref in ((0, next_ref), (1, prev_ref)):
        hot = jnp.where(index_ref[place : place + 1, :] == rows, 1.0, 0.0)
        total = total + dot(hot, ref[...].astype(jnp.float32))
    out_ref[...] = total.astype(jnp.bfloat16)


def settle(base, from_next, from_prev, index):
    return pl.pallas_call(
        settle_kernel,
        in_specs=[VMEM] * 4,
        out_specs=VMEM,
        out_shape=jax.ShapeDtypeStruct(base.shape, jnp.bfloat16),
        compiler_params=PARAMS,
        name="settle_ghosts",
    )(base, from_next, from_prev, index)


def together(*values):
    return lax.optimization_barrier(values)


CORES = [(i, i ^ 1) for i in range(8)]
BESIDE = [(2 * z + c, 2 * (z ^ 1) + c) for z in range(4) for c in range(2)]
OPPOSITE = [(2 * z + c, 2 * (3 - z) + c) for z in range(4) for c in range(2)]


def add(*parts):
    return sum(part.astype(jnp.float32) for part in parts).astype(jnp.bfloat16)


def mixed_general(mixture, own):
    per_group = own.shape[0]
    columns = lax.dynamic_slice_in_dim(mixture, lax.axis_index("dp") * per_group, per_group, 1)
    sums = jnp.einsum(
        "se,erk->srk", columns, own.astype(jnp.float32), precision=lax.Precision.HIGHEST
    ).astype(jnp.bfloat16)
    return lax.psum_scatter(sums, "dp", scatter_dimension=0, tiled=False)


def to_peer(array, spaces, k):
    return lax.ppermute(array, "space", [(i, i ^ k) for i in range(spaces)])


def on_device(
    features,
    grad_out,
    wigner,
    sources,
    targets,
    ghost_index,
    edge_count,
    mixture,
    w_zero,
    w_one,
    w_two,
):
    edges = sources.shape[0]
    own_rows = features.shape[0]
    ghosts = ghost_index.shape[2]
    spaces = lax.axis_size("space")
    place = jnp.stack([lax.axis_index("dp"), lax.axis_index("space")]).astype(jnp.int32)
    up = [(i, (i + 1) % spaces) for i in range(spaces)]
    down = [(j, i) for i, j in up]
    per_group, rows_zero = w_zero.shape[:2]
    rows_one, rows_two = w_one.shape[2], w_two.shape[2]
    sources = sources.reshape(1, edges)
    targets = targets.reshape(1, edges)
    w_one = w_one.reshape(per_group, -1, w_one.shape[-1])
    w_two = w_two.reshape(per_group, -1, w_two.shape[-1])
    scale = float(edges * spaces) ** (-0.5)

    def frames(from_prev, from_next):
        return enter(
            place,
            edge_count,
            features,
            jnp.concatenate([from_prev, from_next], 0),
            grad_out,
            sources,
            targets,
            wigner,
            spaces,
        )

    to_next, to_prev = pick_ghosts(ghost_index, features)

    if lax.axis_size("dp") == 8 and spaces == 4:
        half = rows_zero // 2
        chunks = [
            (0, w_zero, 0, half, (0, 1, 0)),
            (3, w_two, 0, 2 * rows_two, (0, 2, 0)),
            (1, w_one, 0, rows_one, (0, 1, 0)),
            (1, w_one, rows_one, rows_one, (1, 1, 0)),
            (0, w_zero, half, rows_zero - half, (0, 1, half)),
        ]

        def swap_cores(array):
            return lax.ppermute(array, "dp", CORES)

        def mix_chunk(j, other, other_first=0):
            _, own, first, rows, _ = chunks[j]
            return mix(place, mixture, own, other, first, other_first, rows)

        def swap_beside(both):
            return lax.ppermute(both, "dp", BESIDE)

        def total_opposite(j, across, beside):
            return add(across, beside[chunks[j][3] :])

        def swap_opposite(total):
            return lax.ppermute(total, "dp", OPPOSITE)

        def total_here(j, here, beside, opposite):
            return add(here, beside[: chunks[j][3]], opposite)

        def to_sides(shard):
            return to_peer(shard, spaces, 1), to_peer(shard, spaces, 2)

        def forward(j, sides):
            along = 1 if j == 1 else 2
            return to_peer(sides[(3 ^ along) - 1], spaces, along)

        def pieces(j, shard, sides, last, at=None):
            _, _, _, rows, (part, parts, offset) = chunks[j]
            return [
                ((k, part, parts, offset, rows // parts, at), a)
                for k, a in enumerate((shard, *sides, last))
            ]

        other0 = swap_cores(w_zero)
        other0, to_next, to_prev = together(other0, to_next, to_prev)
        both0, across0, here0 = mix_chunk(0, other0)
        beside0 = swap_beside(both0)
        from_prev = lax.ppermute(to_next, "space", up)
        from_next = lax.ppermute(to_prev, "space", down)
        sent, other0 = together(w_two, other0)
        other1 = swap_cores(sent)
        raw = pack_inputs(edge_count, grad_out, targets, wigner)
        raws = [to_peer(raw, spaces, 1), to_peer(raw, spaces, 2)]
        both1, across1, here1 = mix_chunk(1, other1)
        beside1 = swap_beside(both1)
        beside0, here1, from_prev, from_next = together(beside0, here1, from_prev, from_next)
        total0 = total_opposite(0, across0, beside0)
        opposite0 = swap_opposite(total0)
        sent, other1, here1 = together(w_one, other1, here1)
        other2 = swap_cores(sent)
        total0, from_prev, from_next = together(total0, from_prev, from_next)
        frame, back, *slabs = frames(from_prev, from_next)
        slabs[1], slabs[2], other2 = together(slabs[1], slabs[2], other2)
        slabs[1], slabs[2] = to_peer(slabs[1], spaces, 1), to_peer(slabs[2], spaces, 2)
        raw, frame, *raws = together(raw, frame, *raws)
        raws.append(to_peer(raw, spaces, 3))
        other2, frame = together(other2, frame)
        both2, across2, here2 = mix_chunk(2, other2)
        both3, across3, here3 = mix_chunk(3, other2, rows_one)
        both2, here2, here3, opposite0 = together(both2, here2, here3, opposite0)
        beside2 = swap_beside(both2)
        here3, raws[2] = together(here3, raws[2])
        backs = peer_frames(raws, own_rows, wigner.shape[0])
        beside1, here2, here3, backs = together(beside1, here2, here3, backs)
        beside1, *slabs[1:] = together(beside1, *slabs[1:])
        slabs[3] = to_peer(slabs[3], spaces, 3)
        total1 = total_opposite(1, across1, beside1)
        opposite1 = swap_opposite(total1)
        other0, beside1 = together(other0, beside1)
        both4, across4, here4 = mix_chunk(4, other0, half)
        both3, beside2, here4, slabs[3] = together(both3, beside2, here4, slabs[3])
        beside3 = swap_beside(both3)
        total2 = total_opposite(2, across2, beside2)
        opposite2 = swap_opposite(total2)
        opposite1, beside2 = together(opposite1, beside2)
        shard1 = finish((here0, beside0, opposite0), (here1, beside1, opposite1))
        sides1 = to_sides(shard1)
        both4, beside3, shard1 = together(both4, beside3, shard1)
        beside4 = swap_beside(both4)
        total3 = total_opposite(3, across3, beside3)
        opposite3 = swap_opposite(total3)
        shard2 = total_here(2, here2, beside2, opposite2)
        shard2, *sides1 = together(shard2, *sides1)
        forward1 = forward(1, sides1)
        sides2 = to_sides(shard2)
        beside4, shard2, slabs[3] = together(beside4, shard2, slabs[3])
        total4 = total_opposite(4, across4, beside4)
        opposite4 = swap_opposite(total4)
        opposite3, total4 = together(opposite3, total4)
        shard3 = total_here(3, here3, beside3, opposite3)
        sides3 = to_sides(shard3)
        late_back, beside4 = together(back, beside4)
        grad_mix = weight_grads(late_back, backs, slabs, scale)
        opposite4, *grad_mix = together(opposite4, *grad_mix)
        opposite4, *sides2 = together(opposite4, *sides2)
        shard4 = total_here(4, here4, beside4, opposite4)
        sides4 = to_sides(shard4)
        forward2 = forward(2, sides2)
        shard4 = total_here(4, here4, beside4, opposite4)
        sides4 = to_sides(shard4)
        outs, grads = {}, {}
        whole = {
            3: pieces(1, shard1, sides1, forward1, half * BLOCK_COUNTS[0]),
            1: pieces(2, shard2, sides2, forward2) + pieces(3, shard3, sides3, forward(3, sides3)),
            0: pieces(0, shard1, sides1, forward1, 0) + pieces(4, shard4, sides4, to_peer(shard4, spaces, 3)),
        }
    else:
        from_prev = lax.ppermute(to_next, "space", up)
        from_next = lax.ppermute(to_prev, "space", down)
        frame, back, *slabs = frames(from_prev, from_next)
        slabs = [slabs[0]] + [to_peer(slabs[k], spaces, k) for k in range(1, spaces)]
        raw = pack_inputs(edge_count, grad_out, targets, wigner)
        raws = [to_peer(raw, spaces, k) for k in range(1, spaces)]
        backs = peer_frames(raws, own_rows, wigner.shape[0])
        grad_mix = weight_grads(back, backs, slabs, scale)
        outs, grads, whole = {}, {}, {}
        for group, own, parts in ((3, w_two, 2), (1, w_one, 2), (0, w_zero, 1)):
            shard = mixed_general(mixture, own)
            rows = shard.shape[0] // parts

            def place_of(k):
                return (k, 0, parts, 0, rows, None)

            whole[group] = [(place_of(0), shard)] + [
                (place_of(k), to_peer(shard, spaces, k)) for k in range(1, spaces)
            ]

    for group, pieces_of in whole.items():
        if group == 0:
            frame, grads[1] = together(frame, grads[1])
        outs[group], grads[group] = apply_weights(group, place, frame, back, pieces_of, spaces)
    base, returning = leave_back(
        [grads[g] for g in (0, 1, 3)], wigner, sources, grad_out, 2 * ghosts
    )
    back_next = lax.ppermute(returning[:ghosts], "space", down)
    back_prev = lax.ppermute(returning[ghosts:], "space", up)
    updated = leave_forward([outs[g] for g in (0, 1, 3)], wigner, edge_count, targets, features)
    grad_features = settle(base, back_next, back_prev, ghost_index[0])
    grad_mix0, grad_mix1, grad_mix2 = grad_mix
    return (updated, grad_features, grad_mix0[None], grad_mix1[None], grad_mix2[None])


def solution(mesh):
    return jax.shard_map(
        on_device,
        mesh=mesh,
        in_specs=(
            P(("dp", "space"), None),
            P(("dp", "space"), None),
            P(None, ("dp", "space")),
            P(("dp", "space")),
            P(("dp", "space")),
            P(("dp", "space"), None, None),
            P("dp", "space"),
            P(),
            P("dp", "space", None),
            P("dp", None, "space", None),
            P("dp", None, "space", None),
        ),
        out_specs=(
            P(("dp", "space"), None),
            P(("dp", "space"), None),
            P("dp", "space", None),
            P("dp", None, "space", None),
            P("dp", None, "space", None),
        ),
        check_vma=False,
    )
```

```python
import functools

import jax
import jax.numpy as jnp
from jax import lax
from jax.experimental import pallas as pl
from jax.experimental.pallas import tpu as pltpu
from jax.sharding import PartitionSpec as P

CHANNELS = 128
LMAX = 6
MMAX = 2
MESSAGE_SCALE = 0.25

BLOCK_COUNTS = (LMAX + 1, LMAX, LMAX, LMAX - 1, LMAX - 1)
FRAME_BLOCKS = sum(BLOCK_COUNTS)
FRAME_W = FRAME_BLOCKS * CHANNELS
COEFFS = (LMAX + 1) ** 2
NODE_W = COEFFS * CHANNELS

NN = (((1,), (0,)), ((), ()))
NT = (((1,), (1,)), ((), ()))
TN = (((0,), (0,)), ((), ()))

PARAMS = pltpu.CompilerParams(vmem_limit_bytes=48 * 1024 * 1024)
VMEM = pl.BlockSpec(memory_space=pltpu.VMEM)
SMEM = pl.BlockSpec(memory_space=pltpu.SMEM)
ANY = pl.BlockSpec(memory_space=pl.ANY)
HBM = pl.BlockSpec(memory_space=pltpu.HBM)


def dot(a, b, dims=NN):
    return lax.dot_general(a, b, dims, preferred_element_type=jnp.float32)


def degree_start(degree):
    return degree * (2 * degree - 1) * (2 * degree + 1) // 3


def frame_block(degree, order):
    if order == 0:
        return degree
    group = 2 * abs(order) - (1 if order > 0 else 0)
    return sum(BLOCK_COUNTS[:group]) + degree - abs(order)


def identity():
    rows = lax.broadcasted_iota(jnp.int32, (CHANNELS, CHANNELS), 0)
    cols = lax.broadcasted_iota(jnp.int32, (CHANNELS, CHANNELS), 1)
    return jnp.where(rows == cols, 1.0, 0.0).astype(jnp.bfloat16)


def mix_kernel(offset, other_offset, place_ref, mixture_ref, own_ref, other_ref, *refs):
    (both, across, here), (own, other, sems) = refs[:3], refs[3:]
    per_group, rows, width = own.shape
    outs = (both.at[:rows], both.at[rows:], across, here)
    blocks = sems.shape[1]
    block = rows // blocks
    copies = []
    for b in range(blocks):
        span = pl.ds(b * block, block)
        source = pl.ds(offset + b * block, block)
        copies.append(
            (
                pltpu.make_async_copy(own_ref.at[:, source, :], own.at[:, span, :], sems.at[0, b]),
                pltpu.make_async_copy(
                    other_ref.at[:, pl.ds(other_offset + b * block, block), :],
                    other.at[:, span, :],
                    sems.at[1, b],
                ),
            )
        )
    for pair in copies:
        for copy in pair:
            copy.start()
    dp = place_ref[0]
    z = dp // 2
    core = dp % 2
    beside = z + 1 - 2 * (z % 2)
    dests = (beside, 3 - beside, 3 - z, z)
    partner = dp + 1 - 2 * core
    coefs = []
    for dest in dests:
        system = 2 * dest + core
        coefs.append(
            [mixture_ref[system, dp * per_group + e] for e in range(per_group)]
            + [mixture_ref[system, partner * per_group + e] for e in range(per_group)]
        )

    def body(step, carry):
        row = pl.multiple_of(step * 16, 16)
        for column in range(0, width, CHANNELS):
            span = pl.ds(column, CHANNELS)
            parts = [own[e, pl.ds(row, 16), span].astype(jnp.float32) for e in range(per_group)]
            parts += [other[e, pl.ds(row, 16), span].astype(jnp.float32) for e in range(per_group)]
            for out, coef in zip(outs, coefs):
                total = coef[0] * parts[0]
                for c, part in zip(coef[1:], parts[1:]):
                    total = total + c * part
                out[pl.ds(row, 16), span] = total.astype(jnp.bfloat16)
        return carry

    for b, pair in enumerate(copies):
        for copy in pair:
            copy.wait()
        lax.fori_loop(b * block // 16, (b + 1) * block // 16, body, 0)


def mix(place, mixture, own, other, offset, other_offset, rows):
    per_group, _, width = other.shape
    blocks = 2 if rows % 32 == 0 else 1
    pair = jax.ShapeDtypeStruct((2 * rows, width), jnp.bfloat16)
    single = jax.ShapeDtypeStruct((rows, width), jnp.bfloat16)
    return pl.pallas_call(
        functools.partial(mix_kernel, offset, other_offset),
        in_specs=[SMEM, SMEM, HBM, ANY],
        out_specs=[VMEM] * 3,
        out_shape=[pair, single, single],
        scratch_shapes=[
            pltpu.VMEM((per_group, rows, width), jnp.bfloat16),
            pltpu.VMEM((per_group, rows, width), jnp.bfloat16),
            pltpu.SemaphoreType.DMA((2, blocks)),
        ],
        compiler_params=PARAMS,
        name="mix",
    )(place, mixture, pltpu.with_memory_space_constraint(own, pltpu.HBM), other)


def pick_kernel(index_ref, features_ref, next_ref, prev_ref):
    own = features_ref.shape[0]
    ghosts = index_ref.shape[2]
    columns = lax.broadcasted_iota(jnp.int32, (ghosts, own), 1)
    for place, out in ((0, next_ref), (1, prev_ref)):
        rows = lax.broadcasted_iota(jnp.int32, (ghosts, own), 0)
        wanted = jnp.zeros((ghosts, own), jnp.int32)
        for g in range(ghosts):
            wanted = jnp.where(rows == g, index_ref[0, place, g], wanted)
        hot = jnp.where(columns == wanted, 1.0, 0.0).astype(jnp.bfloat16)
        out[...] = dot(hot, features_ref[...]).astype(jnp.bfloat16)


def pick_ghosts(index, features):
    out = jax.ShapeDtypeStruct((index.shape[2], features.shape[1]), jnp.bfloat16)
    return pl.pallas_call(
        pick_kernel,
        in_specs=[SMEM, VMEM],
        out_specs=[VMEM] * 2,
        out_shape=[out, out],
        compiler_params=PARAMS,
        name="pick_ghosts",
    )(index, features)


def hot_rows(index, count, values=1.0, start=0):
    rows = lax.broadcasted_iota(jnp.int32, (count, index.shape[1]), 0) + start
    return jnp.where(index == rows, values, 0.0).astype(jnp.bfloat16)


def turn_into(wide, sources, targets):
    step_rows = 32

    def body(step, carry):
        base = pl.multiple_of(step * step_rows, step_rows)
        for degree in range(LMAX + 1):
            extent = 2 * degree + 1
            kept = min(degree, MMAX)
            for order in range(-kept, kept + 1):
                start = degree_start(degree) + extent * (degree + order)
                totals = [0.0] * len(sources)
                for n in range(extent):
                    row = pl.ds((degree * degree + n) * CHANNELS + base, step_rows)
                    factor = wide[pl.ds(start + n, 1), :]
                    totals = [t + factor * s[row, :] for t, s in zip(totals, sources)]
                place = pl.ds(frame_block(degree, order) * CHANNELS + base, step_rows)
                for target, total in zip(targets, totals):
                    target[place, :] = total.astype(jnp.bfloat16)
        return carry

    lax.fori_loop(0, CHANNELS // step_rows, body, 0)


BAND = 16


def packed_rows(own, wigner_rows):
    rotations = COEFFS * own
    targets = rotations + BAND * -(-wigner_rows // BAND)
    return rotations, targets, targets + BAND


def live_targets(count_ref, targets_ref):
    targets = targets_ref[...]
    live = lax.broadcasted_iota(jnp.int32, targets.shape, 1) < count_ref[0, 0]
    return jnp.where(live, targets, -1)


def pack_kernel(count_ref, grad_ref, targets_ref, wigner_ref, out_ref):
    own = grad_ref.shape[0]
    wig_rows, edges = wigner_ref.shape
    rotations_at, targets_at, end = packed_rows(own, wig_rows)
    for n in range(COEFFS):
        out_ref[n * own : (n + 1) * own, :] = grad_ref[:, n * CHANNELS : (n + 1) * CHANNELS]
    padding = jnp.zeros((targets_at - rotations_at - wig_rows, edges), jnp.float32)
    rotations = jnp.concatenate([wigner_ref[...].astype(jnp.float32), padding], 0)
    out_ref[rotations_at:targets_at, :] = rotations.astype(jnp.bfloat16)
    marks = live_targets(count_ref, targets_ref).astype(jnp.float32)
    out_ref[targets_at:end, :] = jnp.broadcast_to(marks, (BAND, edges)).astype(jnp.bfloat16)


def pack_inputs(count, grad_out, targets, wigner):
    rows = packed_rows(grad_out.shape[0], wigner.shape[0])[-1]
    return pl.pallas_call(
        pack_kernel,
        in_specs=[SMEM] + [VMEM] * 3,
        out_specs=VMEM,
        out_shape=jax.ShapeDtypeStruct((rows, wigner.shape[1]), jnp.bfloat16),
        compiler_params=PARAMS,
        name="pack_inputs",
    )(count, grad_out, targets, wigner)


def enter_kernel(
    place_ref, count_ref, features_ref, ghosts_ref, grad_ref, sources_ref, targets_ref, wigner_ref,
    frame_ref, back_ref, *rest,
):
    slabs, (wide, forward, backward, turned, turned_back) = rest[:-5], rest[-5:]
    own = features_ref.shape[0]
    extra = ghosts_ref.shape[0]
    wide[...] = wigner_ref[...].astype(jnp.float32)
    sources = sources_ref[...]
    targets = live_targets(count_ref, targets_ref)
    from_own = hot_rows(sources, own)
    from_ghost = hot_rows(sources, extra, start=own)
    to_own = hot_rows(targets, own, MESSAGE_SCALE)
    for n in range(COEFFS):
        span = pl.ds(n * CHANNELS, CHANNELS)
        forward[span, :] = dot(features_ref[:, span], from_own, TN) + dot(
            ghosts_ref[:, span], from_ghost, TN
        )
        backward[span, :] = dot(grad_ref[:, span], to_own, TN)
    turn_into(wide, (forward, backward), (turned, turned_back))
    eye = identity()
    for k in range(FRAME_BLOCKS):
        span = pl.ds(k * CHANNELS, CHANNELS)
        frame_ref[:, span] = dot(eye, turned[span, :], NT).astype(jnp.bfloat16)
        back_ref[:, span] = dot(eye, turned_back[span, :], NT).astype(jnp.bfloat16)
    spaces = len(slabs)
    for peer, slab in enumerate(slabs):
        position = lax.bitwise_xor(place_ref[1], jnp.int32(peer))
        at = first = 0
        for blocks in BLOCK_COUNTS:
            rows = blocks * CHANNELS // spaces
            begin = pl.multiple_of(first + position * rows, BAND)
            slab[at : at + rows, :] = turned[pl.ds(begin, rows), :]
            at += rows
            first += blocks * CHANNELS


def enter(place, count, features, ghosts, grad_out, sources, targets, wigner, spaces):
    edges = sources.shape[1]
    frame = jax.ShapeDtypeStruct((edges, FRAME_W), jnp.bfloat16)
    slab = jax.ShapeDtypeStruct((FRAME_W // spaces, edges), jnp.bfloat16)
    return pl.pallas_call(
        enter_kernel,
        in_specs=[SMEM, SMEM] + [VMEM] * 6,
        out_specs=[VMEM] * (2 + spaces),
        out_shape=[frame, frame] + [slab] * spaces,
        scratch_shapes=[
            pltpu.VMEM((wigner.shape[0], edges), jnp.float32),
            pltpu.VMEM((NODE_W, edges), jnp.float32),
            pltpu.VMEM((NODE_W, edges), jnp.float32),
            pltpu.VMEM((FRAME_W, edges), jnp.bfloat16),
            pltpu.VMEM((FRAME_W, edges), jnp.bfloat16),
        ],
        compiler_params=PARAMS,
        name="enter_frame",
    )(place, count, features, ghosts, grad_out, sources, targets, wigner)


def peer_frames_kernel(own, wig_rows, *refs):
    packs, (out, wide, backward, turned_back) = refs[:-4], refs[-4:]
    rotations_at, targets_at, end = packed_rows(own, wig_rows)
    eye = identity()
    for peer, pack in enumerate(packs):
        wide[...] = pack[rotations_at:targets_at, :].astype(jnp.float32)
        targets = pack[targets_at:end, :].astype(jnp.float32)[:1].astype(jnp.int32)
        to_own = hot_rows(targets, own, MESSAGE_SCALE)
        for n in range(COEFFS):
            backward[n * CHANNELS : (n + 1) * CHANNELS, :] = dot(
                pack[n * own : (n + 1) * own, :], to_own, TN
            )
        turn_into(wide, (backward,), (turned_back,))
        for k in range(FRAME_BLOCKS):
            span = pl.ds(k * CHANNELS, CHANNELS)
            out[peer, :, span] = dot(eye, turned_back[span, :], NT).astype(jnp.bfloat16)


def peer_frames(packs, own, wig_rows):
    edges = packs[0].shape[1]
    return pl.pallas_call(
        functools.partial(peer_frames_kernel, own, wig_rows),
        in_specs=[VMEM] * len(packs),
        out_specs=VMEM,
        out_shape=jax.ShapeDtypeStruct((len(packs), edges, FRAME_W), jnp.bfloat16),
        scratch_shapes=[
            pltpu.VMEM((BAND * -(-wig_rows // BAND), edges), jnp.float32),
            pltpu.VMEM((NODE_W, edges), jnp.float32),
            pltpu.VMEM((FRAME_W, edges), jnp.bfloat16),
        ],
        compiler_params=PARAMS,
        name="peer_frames",
    )(*packs)


def weight_grad_kernel(scale, back_ref, backs, *refs):
    all_slabs, (out_zero, out_one, out_two) = refs[:-3], refs[-3:]
    spaces = len(all_slabs)
    all_backs = [back_ref] + [backs.at[k] for k in range(spaces - 1)]
    rows = [blocks * CHANNELS // spaces for blocks in BLOCK_COUNTS]
    widths = [blocks * CHANNELS for blocks in BLOCK_COUNTS]

    def product(a, b):
        left = slice(sum(rows[:a]), sum(rows[: a + 1]))
        right = slice(sum(widths[:b]), sum(widths[: b + 1]))
        return sum(dot(s[left, :], d[:, right]) for s, d in zip(all_slabs, all_backs))

    out_zero[...] = (scale * product(0, 0)).astype(jnp.bfloat16)
    for out, group in ((out_one, 1), (out_two, 3)):
        out[0] = (scale * (product(group, group) + product(group + 1, group + 1))).astype(jnp.bfloat16)
        out[1] = (scale * (product(group, group + 1) - product(group + 1, group))).astype(jnp.bfloat16)


def weight_grads(back, backs, slabs, scale):
    spaces = len(slabs)
    k0, k1, _, k2, _ = [blocks * CHANNELS for blocks in BLOCK_COUNTS]
    return pl.pallas_call(
        functools.partial(weight_grad_kernel, scale),
        in_specs=[VMEM] * (2 + spaces),
        out_specs=[VMEM] * 3,
        out_shape=[
            jax.ShapeDtypeStruct((k0 // spaces, k0), jnp.bfloat16),
            jax.ShapeDtypeStruct((2, k1 // spaces, k1), jnp.bfloat16),
            jax.ShapeDtypeStruct((2, k2 // spaces, k2), jnp.bfloat16),
        ],
        compiler_params=PARAMS,
        name="weight_grads",
    )(back, backs, *slabs)


def apply_kernel(group, places, local_rows, place_ref, frame_ref, back_ref, *refs):
    shards, (out_ref, grad_ref, full) = refs[:-3], refs[-3:]
    parts = 1 if group == 0 else 2
    for (peer, first_part, count, offset, rows, at), shard in zip(places, shards):
        position = lax.bitwise_xor(place_ref[1], jnp.int32(peer))
        begin = pl.multiple_of(position * local_rows + offset, 16)
        for k in range(count):
            if at is None:
                full[first_part + k, pl.ds(begin, rows), :] = shard[k * rows : (k + 1) * rows, :]
                continue
            for column in range(BLOCK_COUNTS[group]):
                full[
                    first_part + k,
                    pl.ds(begin, rows),
                    column * CHANNELS : (column + 1) * CHANNELS,
                ] = shard[at : at + rows, :]
                at += rows
    first = sum(BLOCK_COUNTS[:group]) * CHANNELS
    width = BLOCK_COUNTS[group] * CHANNELS
    eye = identity()
    edges = frame_ref.shape[0]

    def put_turned(value, offset):
        value = value.astype(jnp.bfloat16)
        for k in range(0, width, CHANNELS):
            out_ref[offset + k : offset + k + CHANNELS, :] = dot(
                eye, value[:, k : k + CHANNELS], NT
            ).astype(jnp.bfloat16)

    if parts == 1:
        grad_ref[...] = dot(full[0], back_ref[:, first : first + width], NT).astype(jnp.bfloat16)
        put_turned(dot(frame_ref[:, first : first + width], full[0]), 0)
        return
    second = first + width
    back = jnp.concatenate([back_ref[:, first:second], back_ref[:, second : second + width]], 0)
    real = dot(full[0], back, NT)
    imag = dot(full[1], back, NT)
    grad_ref[:width, :] = (real[:, :edges] + imag[:, edges:]).astype(jnp.bfloat16)
    grad_ref[width:, :] = (real[:, edges:] - imag[:, :edges]).astype(jnp.bfloat16)
    frame = jnp.concatenate([frame_ref[:, first:second], frame_ref[:, second : second + width]], 0)
    real = dot(frame, full[0])
    imag = dot(frame, full[1])
    put_turned(real[:edges] - imag[edges:], 0)
    put_turned(imag[:edges] + real[edges:], width)


def apply_weights(group, place, frame, back, pieces, spaces):
    places, shards = zip(*pieces)
    edges = frame.shape[0]
    width = BLOCK_COUNTS[group] * CHANNELS
    parts = 1 if group == 0 else 2
    out = jax.ShapeDtypeStruct((parts * width, edges), jnp.bfloat16)
    return pl.pallas_call(
        functools.partial(apply_kernel, group, places, width // spaces),
        in_specs=[SMEM] + [VMEM] * (2 + len(shards)),
        out_specs=[VMEM] * 2,
        out_shape=[out, out],
        scratch_shapes=[pltpu.VMEM((parts, width, width), jnp.bfloat16)],
        compiler_params=PARAMS,
        name=f"apply_weights_{group}",
    )(place, frame, back, *shards)


def finish_kernel(*refs):
    out = refs[-1]
    at = 0
    for here, beside, opposite in zip(refs[:-1:3], refs[1:-1:3], refs[2:-1:3]):
        rows, width = here.shape
        step = rows if rows < 160 else rows // 2
        for first in range(0, rows, step):
            span = slice(first, first + step)
            for column in range(0, width, CHANNELS):
                lanes = slice(column, column + CHANNELS)
                total = sum(r[span, lanes].astype(jnp.float32) for r in (here, beside, opposite))
                out[at : at + step, :] = total.astype(jnp.bfloat16)
                at += step


def finish(*chunks):
    arrays = [array for chunk in chunks for array in chunk]
    rows = sum(here.size // CHANNELS for here, _, _ in chunks)
    return pl.pallas_call(
        finish_kernel,
        in_specs=[VMEM] * len(arrays),
        out_specs=VMEM,
        out_shape=jax.ShapeDtypeStruct((rows, CHANNELS), jnp.bfloat16),
        compiler_params=PARAMS,
        name="finish_first",
    )(*arrays)


def leave(frames, wigner_ref, wide, turned):
    wide[...] = wigner_ref[...].astype(jnp.float32)
    step_rows = 32

    def body(step, carry):
        base = pl.multiple_of(step * step_rows, step_rows)
        for degree in range(LMAX + 1):
            extent = 2 * degree + 1
            kept = min(degree, MMAX)
            values = []
            for order in range(-kept, kept + 1):
                source = frames[abs(order)]
                block = degree - abs(order)
                if order < 0:
                    block += BLOCK_COUNTS[2 * -order]
                values.append(
                    source[pl.ds(block * CHANNELS + base, step_rows), :].astype(jnp.float32)
                )
            for n in range(extent):
                total = 0.0
                for order, value in zip(range(-kept, kept + 1), values):
                    start = degree_start(degree) + extent * (degree + order) + n
                    total = total + wide[pl.ds(start, 1), :] * value
                row = pl.ds((degree * degree + n) * CHANNELS + base, step_rows)
                turned[row, :] = total.astype(jnp.bfloat16)
        return carry

    lax.fori_loop(0, CHANNELS // step_rows, body, 0)


def leave_back_kernel(
    zero_ref, one_ref, two_ref, wigner_ref, sources_ref, grad_ref, base_ref, ghost_ref, wide, turned
):
    leave((zero_ref, one_ref, two_ref), wigner_ref, wide, turned)
    own = grad_ref.shape[0]
    extra = ghost_ref.shape[0]
    edges = sources_ref.shape[1]
    rows = lax.broadcasted_iota(jnp.int32, (own + extra, edges), 0)
    hot = jnp.where(sources_ref[...] == rows, 1.0, 0.0).astype(jnp.bfloat16)
    for n in range(COEFFS):
        span = pl.ds(n * CHANNELS, CHANNELS)
        table = dot(hot, turned[span, :], NT)
        base_ref[:, span] = grad_ref[:, span].astype(jnp.float32) + table[:own]
        ghost_ref[:, span] = table[own:].astype(jnp.bfloat16)


def leave_kernel(
    zero_ref, one_ref, two_ref, wigner_ref, count_ref, targets_ref, features_ref, out_ref, wide, turned
):
    leave((zero_ref, one_ref, two_ref), wigner_ref, wide, turned)
    own = features_ref.shape[0]
    edges = targets_ref.shape[1]
    rows = lax.broadcasted_iota(jnp.int32, (own, edges), 0)
    live = lax.broadcasted_iota(jnp.int32, (own, edges), 1) < count_ref[0, 0]
    hot = jnp.where((targets_ref[...] == rows) & live, MESSAGE_SCALE, 0.0).astype(jnp.bfloat16)
    for n in range(COEFFS):
        span = pl.ds(n * CHANNELS, CHANNELS)
        out_ref[:, span] = (
            features_ref[:, span].astype(jnp.float32) + dot(hot, turned[span, :], NT)
        ).astype(jnp.bfloat16)


def leave_scratch(wigner):
    rows, edges = wigner.shape
    return [pltpu.VMEM((rows, edges), jnp.float32), pltpu.VMEM((NODE_W, edges), jnp.bfloat16)]


def leave_back(frames, wigner, sources, grad_out, extra):
    own = grad_out.shape[0]
    return pl.pallas_call(
        leave_back_kernel,
        in_specs=[VMEM] * 6,
        out_specs=[VMEM] * 2,
        out_shape=[
            jax.ShapeDtypeStruct((own, NODE_W), jnp.float32),
            jax.ShapeDtypeStruct((extra, NODE_W), jnp.bfloat16),
        ],
        scratch_shapes=leave_scratch(wigner),
        compiler_params=PARAMS,
        name="leave_frame_back",
    )(*frames, wigner, sources, grad_out)


def leave_forward(frames, wigner, count, targets, features):
    return pl.pallas_call(
        leave_kernel,
        in_specs=[VMEM] * 4 + [SMEM] + [VMEM] * 2,
        out_specs=VMEM,
        out_shape=jax.ShapeDtypeStruct(features.shape, jnp.bfloat16),
        scratch_shapes=leave_scratch(wigner),
        compiler_params=PARAMS,
        name="leave_frame",
    )(*frames, wigner, count, targets, features)


def settle_kernel(base_ref, next_ref, prev_ref, index_ref, out_ref):
    own = base_ref.shape[0]
    ghosts = next_ref.shape[0]
    rows = lax.broadcasted_iota(jnp.int32, (own, ghosts), 0)
    total = base_ref[...]
    for place, ref in ((0, next_ref), (1, prev_ref)):
        hot = jnp.where(index_ref[place : place + 1, :] == rows, 1.0, 0.0)
        total = total + dot(hot, ref[...].astype(jnp.float32))
    out_ref[...] = total.astype(jnp.bfloat16)


def settle(base, from_next, from_prev, index):
    return pl.pallas_call(
        settle_kernel,
        in_specs=[VMEM] * 4,
        out_specs=VMEM,
        out_shape=jax.ShapeDtypeStruct(base.shape, jnp.bfloat16),
        compiler_params=PARAMS,
        name="settle_ghosts",
    )(base, from_next, from_prev, index)


def together(*values):
    return lax.optimization_barrier(values)


CORES = [(i, i ^ 1) for i in range(8)]
BESIDE = [(2 * z + c, 2 * (z ^ 1) + c) for z in range(4) for c in range(2)]
OPPOSITE = [(2 * z + c, 2 * (3 - z) + c) for z in range(4) for c in range(2)]


def add(*parts):
    return sum(part.astype(jnp.float32) for part in parts).astype(jnp.bfloat16)


def mixed_general(mixture, own):
    per_group = own.shape[0]
    columns = lax.dynamic_slice_in_dim(mixture, lax.axis_index("dp") * per_group, per_group, 1)
    sums = jnp.einsum(
        "se,erk->srk", columns, own.astype(jnp.float32), precision=lax.Precision.HIGHEST
    ).astype(jnp.bfloat16)
    return lax.psum_scatter(sums, "dp", scatter_dimension=0, tiled=False)


def to_peer(array, spaces, k):
    return lax.ppermute(array, "space", [(i, i ^ k) for i in range(spaces)])


def on_device(
    features,
    grad_out,
    wigner,
    sources,
    targets,
    ghost_index,
    edge_count,
    mixture,
    w_zero,
    w_one,
    w_two,
):
    edges = sources.shape[0]
    own_rows = features.shape[0]
    ghosts = ghost_index.shape[2]
    spaces = lax.axis_size("space")
    place = jnp.stack([lax.axis_index("dp"), lax.axis_index("space")]).astype(jnp.int32)
    up = [(i, (i + 1) % spaces) for i in range(spaces)]
    down = [(j, i) for i, j in up]
    per_group, rows_zero = w_zero.shape[:2]
    rows_one, rows_two = w_one.shape[2], w_two.shape[2]
    sources = sources.reshape(1, edges)
    targets = targets.reshape(1, edges)
    w_one = w_one.reshape(per_group, -1, w_one.shape[-1])
    w_two = w_two.reshape(per_group, -1, w_two.shape[-1])
    scale = float(edges * spaces) ** (-0.5)

    def frames(from_prev, from_next):
        return enter(
            place,
            edge_count,
            features,
            jnp.concatenate([from_prev, from_next], 0),
            grad_out,
            sources,
            targets,
            wigner,
            spaces,
        )

    to_next, to_prev = pick_ghosts(ghost_index, features)

    if lax.axis_size("dp") == 8 and spaces == 4:
        half = rows_zero // 2
        chunks = [
            (0, w_zero, 0, half, (0, 1, 0)),
            (3, w_two, 0, 2 * rows_two, (0, 2, 0)),
            (1, w_one, 0, rows_one, (0, 1, 0)),
            (1, w_one, rows_one, rows_one, (1, 1, 0)),
            (0, w_zero, half, rows_zero - half, (0, 1, half)),
        ]

        def swap_cores(array):
            return lax.ppermute(array, "dp", CORES)

        def mix_chunk(j, other, other_first=0):
            _, own, first, rows, _ = chunks[j]
            return mix(place, mixture, own, other, first, other_first, rows)

        def swap_beside(both):
            return lax.ppermute(both, "dp", BESIDE)

        def total_opposite(j, across, beside):
            return add(across, beside[chunks[j][3] :])

        def swap_opposite(total):
            return lax.ppermute(total, "dp", OPPOSITE)

        def total_here(j, here, beside, opposite):
            return add(here, beside[: chunks[j][3]], opposite)

        def to_sides(shard):
            return to_peer(shard, spaces, 1), to_peer(shard, spaces, 2)

        def forward(j, sides):
            along = 1 if j == 1 else 2
            return to_peer(sides[(3 ^ along) - 1], spaces, along)

        def pieces(j, shard, sides, last, at=None):
            _, _, _, rows, (part, parts, offset) = chunks[j]
            return [
                ((k, part, parts, offset, rows // parts, at), a)
                for k, a in enumerate((shard, *sides, last))
            ]

        other0 = swap_cores(w_zero)
        other0, to_next, to_prev = together(other0, to_next, to_prev)
        both0, across0, here0 = mix_chunk(0, other0)
        beside0 = swap_beside(both0)
        from_prev = lax.ppermute(to_next, "space", up)
        from_next = lax.ppermute(to_prev, "space", down)
        sent, other0 = together(w_two, other0)
        other1 = swap_cores(sent)
        raw = pack_inputs(edge_count, grad_out, targets, wigner)
        raws = [to_peer(raw, spaces, 1), to_peer(raw, spaces, 2)]
        both1, across1, here1 = mix_chunk(1, other1)
        beside1 = swap_beside(both1)
        beside0, here1, from_prev, from_next = together(beside0, here1, from_prev, from_next)
        total0 = total_opposite(0, across0, beside0)
        opposite0 = swap_opposite(total0)
        sent, other1, here1 = together(w_one, other1, here1)
        other2 = swap_cores(sent)
        total0, from_prev, from_next = together(total0, from_prev, from_next)
        frame, back, *slabs = frames(from_prev, from_next)
        slabs[1], slabs[2], other2 = together(slabs[1], slabs[2], other2)
        slabs[1], slabs[2] = to_peer(slabs[1], spaces, 1), to_peer(slabs[2], spaces, 2)
        raw, frame, *raws = together(raw, frame, *raws)
        raws.append(to_peer(raw, spaces, 3))
        other2, frame = together(other2, frame)
        both2, across2, here2 = mix_chunk(2, other2)
        both3, across3, here3 = mix_chunk(3, other2, rows_one)
        beside2 = swap_beside(both2)
        here3, raws[2] = together(here3, raws[2])
        backs = peer_frames(raws, own_rows, wigner.shape[0])
        beside1, here2, here3, backs, opposite0 = together(beside1, here2, here3, backs, opposite0)
        beside1, *slabs[1:] = together(beside1, *slabs[1:])
        slabs[3] = to_peer(slabs[3], spaces, 3)
        total1 = total_opposite(1, across1, beside1)
        opposite1 = swap_opposite(total1)
        other0, beside1 = together(other0, beside1)
        both4, across4, here4 = mix_chunk(4, other0, half)
        both3, beside2, here4, slabs[3] = together(both3, beside2, here4, slabs[3])
        beside3 = swap_beside(both3)
        total2 = total_opposite(2, across2, beside2)
        opposite2 = swap_opposite(total2)
        opposite1, beside2 = together(opposite1, beside2)
        shard1 = finish((here0, beside0, opposite0), (here1, beside1, opposite1))
        sides1 = to_sides(shard1)
        both4, beside3, shard1 = together(both4, beside3, shard1)
        beside4 = swap_beside(both4)
        total3 = total_opposite(3, across3, beside3)
        opposite3 = swap_opposite(total3)
        shard2 = total_here(2, here2, beside2, opposite2)
        shard2, *sides1 = together(shard2, *sides1)
        forward1 = forward(1, sides1)
        sides2 = to_sides(shard2)
        beside4, shard2, slabs[3] = together(beside4, shard2, slabs[3])
        total4 = total_opposite(4, across4, beside4)
        opposite4 = swap_opposite(total4)
        opposite3, total4 = together(opposite3, total4)
        shard3 = total_here(3, here3, beside3, opposite3)
        shard3, *sides2 = together(shard3, *sides2)
        sides3 = to_sides(shard3)
        forward2 = forward(2, sides2)
        shard4 = total_here(4, here4, beside4, opposite4)
        sides4 = to_sides(shard4)
        last4 = to_peer(shard4, spaces, 3)
        late_back, shard4 = together(back, shard4)
        grad_mix = weight_grads(late_back, backs, slabs, scale)
        shard4, *sides3 = together(shard4, *sides3)
        outs, grads = {}, {}
        whole = {
            3: pieces(1, shard1, sides1, forward1, half * BLOCK_COUNTS[0]),
            1: pieces(2, shard2, sides2, forward2) + pieces(3, shard3, sides3, forward(3, sides3)),
            0: pieces(0, shard1, sides1, forward1, 0) + pieces(4, shard4, sides4, last4),
        }
    else:
        from_prev = lax.ppermute(to_next, "space", up)
        from_next = lax.ppermute(to_prev, "space", down)
        frame, back, *slabs = frames(from_prev, from_next)
        slabs = [slabs[0]] + [to_peer(slabs[k], spaces, k) for k in range(1, spaces)]
        raw = pack_inputs(edge_count, grad_out, targets, wigner)
        raws = [to_peer(raw, spaces, k) for k in range(1, spaces)]
        backs = peer_frames(raws, own_rows, wigner.shape[0])
        grad_mix = weight_grads(back, backs, slabs, scale)
        outs, grads, whole = {}, {}, {}
        for group, own, parts in ((3, w_two, 2), (1, w_one, 2), (0, w_zero, 1)):
            shard = mixed_general(mixture, own)
            rows = shard.shape[0] // parts

            def place_of(k):
                return (k, 0, parts, 0, rows, None)

            whole[group] = [(place_of(0), shard)] + [
                (place_of(k), to_peer(shard, spaces, k)) for k in range(1, spaces)
            ]

    for group, pieces_of in whole.items():
        if group == 0:
            frame, grads[1], *grad_mix = together(frame, grads[1], *grad_mix)
        outs[group], grads[group] = apply_weights(group, place, frame, back, pieces_of, spaces)
    base, returning = leave_back(
        [grads[g] for g in (0, 1, 3)], wigner, sources, grad_out, 2 * ghosts
    )
    back_next = lax.ppermute(returning[:ghosts], "space", down)
    back_prev = lax.ppermute(returning[ghosts:], "space", up)
    updated = leave_forward([outs[g] for g in (0, 1, 3)], wigner, edge_count, targets, features)
    grad_features = settle(base, back_next, back_prev, ghost_index[0])
    grad_mix0, grad_mix1, grad_mix2 = grad_mix
    return (updated, grad_features, grad_mix0[None], grad_mix1[None], grad_mix2[None])


def solution(mesh):
    return jax.shard_map(
        on_device,
        mesh=mesh,
        in_specs=(
            P(("dp", "space"), None),
            P(("dp", "space"), None),
            P(None, ("dp", "space")),
            P(("dp", "space")),
            P(("dp", "space")),
            P(("dp", "space"), None, None),
            P("dp", "space"),
            P(),
            P("dp", "space", None),
            P("dp", None, "space", None),
            P("dp", None, "space", None),
        ),
        out_specs=(
            P(("dp", "space"), None),
            P(("dp", "space"), None),
            P("dp", "space", None),
            P("dp", None, "space", None),
            P("dp", None, "space", None),
        ),
        check_vma=False,
    )
```
